256 devices in a mesh: tgt: 32 (over z, y), qry: 8 (over x, core).
Axes of the slice: x: 4, y: 4, z: 8, core: 2. Of those that a mesh axis runs over, the one named last changes fastest.
Arguments:
- query_feat: bfloat16 [2048, 128], P('qry'), may hold values from -100 to 100
- target_feat: bfloat16 [524288, 128], P('tgt'), may hold values from -15 to 15
- flow_grad: bfloat16 [2048, 2], P('qry'), may hold values from -8 to 8
Outputs:
- grad_query: bfloat16 [2048, 128], P('qry')
- grad_target: bfloat16 [524288, 128], P(('tgt', 'qry'))
The draws below stay inside these ranges and needn't reach their ends.
All inputs are finite; a program needn't handle non-finite values.
Results may differ from the reference program's by a relative error of at most 0.0052.
Values may be sent and summed in bfloat16 or wider, within the bound.
A program may use at most 128 MiB of HBM per device.

```python
import math
import jax
import jax.numpy as jnp
from jax import lax

CHANNELS = 128
FRAME_W = 1024
QUERIES = 2048
TARGETS = 524288


def base_targets(key):
    return 1.8 * jax.random.normal(key, (TARGETS, CHANNELS), jnp.float32)


def draw_target_feat(key, part):
    base = base_targets(key)
    return jnp.clip(base, -15.0, 15.0).astype(jnp.bfloat16)


def draw_query_feat(key, part):
    key = jax.random.fold_in(key, 7)
    values = 1.8 * jax.random.normal(key, (QUERIES, CHANNELS), jnp.float32)
    return jnp.clip(values, -100.0, 100.0).astype(jnp.bfloat16)


def shard_levels(stream_key, shape, split, low, largest):
    loudness, own = 1.0, jax.random.fold_in(stream_key, 6)
    for position, blocks in split:
        draws = jnp.exp(jax.random.uniform(jax.random.fold_in(own, position), (blocks,), jnp.float32, low / len(split), largest / len(split)))
        loudness = loudness * jnp.repeat(draws, shape[position] // blocks).reshape([-1 if axis == position else 1 for axis in range(len(shape))])
    return loudness


def normal_values(stream_key, shape, deviation, bound, split=(), kind=jnp.bfloat16):
    level = shard_levels(stream_key, shape, split, -0.22, 0.18) if split else 1.0
    array = jax.random.normal(stream_key, shape, jnp.float32) * deviation * level
    return jnp.minimum(jnp.maximum(array, -bound), bound).astype(kind)


def setup_inputs(seed: int = 0) -> dict:
    arg_keys = jax.random.split(jax.random.key(seed), 4)
    query_feat = draw_query_feat(jax.random.fold_in(arg_keys[3], 71), 0)
    target_feat = draw_target_feat(jax.random.fold_in(arg_keys[3], 71), 0)
    flow_grad = normal_values(arg_keys[2], (QUERIES, 2), 2.0, 8.0, ((0, 8),))
    return dict(query_feat=query_feat, target_feat=target_feat, flow_grad=flow_grad)


def pixel_coords(index, width):
    column = (index % width).astype(jnp.float32)
    row_pos = (index // width).astype(jnp.float32)
    return ((2.0 * column + 1.0) / width - 1.0, (2.0 * row_pos + 1.0) / width - 1.0)

def reference(query_feat, target_feat, flow_grad):
    scale = 1.0 / math.sqrt(CHANNELS)
    step_len = min(8192, TARGETS)
    count = TARGETS // step_len
    blocks = target_feat.reshape(count, step_len, CHANNELS)
    starts = jnp.arange(count, dtype=jnp.int32) * step_len
    grads = flow_grad.astype(jnp.float32)
    grad_x = grads[:, 0][:, None]
    grad_y = grads[:, 1][:, None]

    def scores_of(block):
        return jnp.dot(query_feat, block.T, preferred_element_type=jnp.float32) * scale

    def stats_step(carry, item):
        peak, total, sum_x, sum_y = carry
        block, begin = item
        scores = scores_of(block)
        coord_x, coord_y = pixel_coords(begin + jnp.arange(step_len, dtype=jnp.int32), FRAME_W)
        top = jnp.maximum(peak, lax.optimization_barrier(jnp.max(scores, axis=1)))
        expo = jnp.exp(scores - top[:, None])
        factor = jnp.exp(peak - top)
        total = total * factor + lax.optimization_barrier(jnp.sum(expo, axis=1))
        sum_x = sum_x * factor + lax.optimization_barrier(jnp.sum(expo * coord_x[None, :], axis=1))
        sum_y = sum_y * factor + lax.optimization_barrier(jnp.sum(expo * coord_y[None, :], axis=1))
        return ((top, total, sum_x, sum_y), None)
    zeros = jnp.zeros((QUERIES,), jnp.float32)
    start_peak = jnp.full((QUERIES,), -jnp.inf, jnp.float32)
    (peak, total, sum_x, sum_y), unused = lax.scan(stats_step, (start_peak, zeros, zeros, zeros), (blocks, starts))
    mean_x = (sum_x / total)[:, None]
    mean_y = (sum_y / total)[:, None]

    def grad_step(acc, item):
        block, begin = item
        scores = scores_of(block)
        coord_x, coord_y = pixel_coords(begin + jnp.arange(step_len, dtype=jnp.int32), FRAME_W)
        prob = jnp.exp(scores - peak[:, None]) / total[:, None]
        inner = grad_x * (coord_x[None, :] - mean_x) + grad_y * (coord_y[None, :] - mean_y)
        dscore = (prob * inner * scale).astype(jnp.bfloat16)
        acc = acc + jnp.dot(dscore, block, preferred_element_type=jnp.float32)
        part = jnp.dot(dscore.T, query_feat, preferred_element_type=jnp.float32)
        return (acc, part)
    acc, parts = lax.scan(grad_step, jnp.zeros((QUERIES, CHANNELS), jnp.float32), (blocks, starts))
    return (acc.astype(jnp.bfloat16), parts.reshape(TARGETS, CHANNELS).astype(jnp.bfloat16))
```

```python
import math

import jax
import jax.numpy as jnp
from jax import lax
from jax.experimental import pallas as pl
from jax.experimental.pallas import tpu as pltpu
from jax.sharding import PartitionSpec as P

MESH = pl.DeviceIdType.MESH
F32, BF16 = jnp.float32, jnp.bfloat16

CHANNELS = 128
FRAME_W = 1024
NQ = 256
NT = 16384
ROWS = NT // FRAME_W
OWN_T = 2048
NZ, NY, NG = 8, 4, 8
PIECE = CHANNELS // NZ
SUB = 256
TILES = SUB // 8
GROUPS = 4
SCALE = 1.0 / math.sqrt(CHANNELS)
LOG2 = SCALE * math.log2(math.e)


def twice(column):
    return jnp.concatenate([column, column], axis=1)


def scores_of(targets, queries):
    return lax.dot_general(targets, queries, (((1,), (1,)), ((), ())), preferred_element_type=F32)


def row_coord(row):
    return (2.0 * row.astype(F32) + 1.0) / FRAME_W - 1.0


def rows_at(start, count):
    return pl.ds(pl.multiple_of(start, count), count)


def kernel(
    q_ref, t_hbm, g_ref, gq_ref, gt_ref,
    t_ref, e_ref, cx_ref, peak_ref, q_all, st_loc, st_y, st_z, coef, v_send, v_recv,
    part_y, piece_z, gt_acc,
    t_sem, q_send, q_recv, y_send, y_recv, z_send, z_recv, c_send, c_recv,
    v_ssem, v_rsem, p_send, p_recv, f_send, f_recv,
):
    tgt, qry = lax.axis_index("tgt"), lax.axis_index("qry")
    z, y = tgt // NY, lax.rem(tgt, NY)

    def z_peer(d):
        return lax.rem(z + d, NZ)

    def y_peer(d):
        return lax.rem(y + d, NY)

    def g_peer(d):
        return lax.rem(qry + d, NG)

    def at_z(d):
        return (z_peer(d) * NY + y, qry)

    def at_y(d):
        return (z * NY + y_peer(d), qry)

    def at_g(d):
        return (tgt, g_peer(d))

    barrier = pltpu.get_barrier_semaphore()
    for d in range(1, NY):
        pl.semaphore_signal(barrier, inc=1, device_id=at_y(d), device_id_type=MESH)
    for d in range(1, NG):
        pl.semaphore_signal(barrier, inc=1, device_id=at_g(d), device_id_type=MESH)
    for d in range(1, NZ):
        pl.semaphore_signal(barrier, inc=1, device_id=at_z(d), device_id_type=MESH)

    def load(i):
        part = rows_at(i * (NT // GROUPS), NT // GROUPS)
        return pltpu.make_async_copy(t_hbm.at[part], t_ref.at[part], t_sem.at[i])

    for i in range(GROUPS):
        load(i).start()

    def remote(src, dst, ssem, rsem, where):
        copy = pltpu.make_async_remote_copy(
            src_ref=src, dst_ref=dst, send_sem=ssem, recv_sem=rsem, device_id=where, device_id_type=MESH
        )
        copy.start()
        return copy

    column = lax.broadcasted_iota(jnp.int32, (FRAME_W, 128), 0)
    cx_ref[...] = row_coord(column)
    queries = q_ref[...]
    grads = g_ref[...].astype(F32)
    grad_x = jnp.broadcast_to(grads[:, 0:1], (NQ, 128)).T[0:1]
    grad_y = jnp.broadcast_to(grads[:, 1:2], (NQ, 128)).T[0:1]

    def stats_row(b, carry):
        peak, total, sum_x, sum_y = carry
        coord_y = row_coord(tgt * ROWS + b)
        for k in range(0, FRAME_W, SUB):
            part = rows_at(b * FRAME_W + k, SUB)
            scores = scores_of(t_ref[part, :], queries).reshape(TILES, 8, NQ)
            top = jnp.maximum(peak, jnp.max(scores, axis=0) * LOG2)
            factor = jnp.exp2(peak - top)
            expo = jnp.exp2(scores * LOG2 - top[None])
            tot = expo[0]
            ahead = tot
            for i in range(1, TILES):
                tot = tot + expo[i]
                ahead = ahead + tot
            x_part = twice(cx_ref[k : k + 8, :]) * tot + (TILES * tot - ahead) * (16.0 / FRAME_W)
            total = total * factor + tot
            sum_x = sum_x * factor + x_part
            sum_y = sum_y * factor + coord_y * tot
            peak = top
            e_ref[part, :] = expo.reshape(SUB, NQ)
            peak_ref[b * (FRAME_W // SUB) + k // SUB] = top
        return peak, total, sum_x, sum_y

    def stats_group(i, carry):
        load(i).wait()
        for r in range(ROWS // GROUPS):
            carry = stats_row(i * (ROWS // GROUPS) + r, carry)
        return carry

    zeros = jnp.zeros((8, NQ), F32)
    carry = (jnp.full((8, NQ), -1e30, F32), zeros, zeros, zeros)
    carry = lax.fori_loop(0, GROUPS // 2, stats_group, carry)

    pl.semaphore_wait(barrier, NY - 1 + NG - 1 + NZ - 1)
    q_copies = [
        remote(q_ref, q_all.at[qry], q_send.at[d], q_recv.at[d], at_g(d)) for d in range(1, NG)
    ]

    carry = lax.fori_loop(GROUPS // 2, GROUPS, stats_group, carry)

    peak8, total8, x8, y8 = carry
    peak_l = jnp.max(peak8, axis=0, keepdims=True)
    factor8 = jnp.exp2(peak8 - peak_l)
    total_l = jnp.sum(total8 * factor8, axis=0, keepdims=True)
    sum_xl = jnp.sum(x8 * factor8, axis=0, keepdims=True)
    sum_yl = jnp.sum(y8 * factor8, axis=0, keepdims=True)
    mean_xl, mean_yl = sum_xl / total_l, sum_yl / total_l

    st_loc[0] = jnp.concatenate([peak_l, total_l, sum_xl, sum_yl, zeros[0:4]], axis=0)
    st_y[y] = st_loc[0]
    y_copies = [
        remote(st_loc.at[0], st_y.at[y], y_send.at[d], y_recv.at[d], at_y(d)) for d in range(1, NY)
    ]

    def grad_row(b, acc):
        coord_y = row_coord(tgt * ROWS + b)
        offset = grad_y * (coord_y - mean_yl)
        parts = []
        for k in range(0, FRAME_W, SUB):
            part = rows_at(b * FRAME_W + k, SUB)
            factor = jnp.exp2(peak_ref[b * (FRAME_W // SUB) + k // SUB] - peak_l)
            expo = (e_ref[part, :].reshape(TILES, 8, NQ) * factor[None]).reshape(SUB, NQ)
            inner = (twice(cx_ref[k : k + SUB, :]) - mean_xl) * grad_x + offset
            parts.append(jnp.concatenate([(expo * inner).astype(BF16), expo.astype(BF16)], axis=1))
        block = t_ref[rows_at(b * FRAME_W, FRAME_W), :]
        return acc + lax.dot_general(
            block, jnp.concatenate(parts, axis=0), (((0,), (0,)), ((), ())), preferred_element_type=F32
        )

    def grad_group(i, acc):
        for r in range(ROWS // GROUPS):
            acc = grad_row(i * (ROWS // GROUPS) + r, acc)
        return acc

    v = lax.fori_loop(0, GROUPS, grad_group, jnp.zeros((CHANNELS, 2 * NQ), F32))

    def merge(slots):
        peak = slots[0][0:1]
        for s in slots[1:]:
            peak = jnp.maximum(peak, s[0:1])
        total = sum_x = sum_y = jnp.zeros((1, NQ), F32)
        for s in slots:
            factor = jnp.exp2(s[0:1] - peak)
            total = total + s[1:2] * factor
            sum_x = sum_x + s[2:3] * factor
            sum_y = sum_y + s[3:4] * factor
        return peak, total, sum_x, sum_y

    for copy in y_copies:
        copy.wait_recv()
    merged = merge([st_y[i] for i in range(NY)])
    st_loc[1] = jnp.concatenate([*merged, peak_l, mean_xl, mean_yl, zeros[0:1]], axis=0)
    st_z[z] = st_loc[1]
    z_copies = [
        remote(st_loc.at[1], st_z.at[z], z_send.at[d], z_recv.at[d], at_z(d)) for d in range(1, NZ)
    ]
    v_send[...] = v.astype(BF16)
    v_recv[z] = v_send[rows_at(z * PIECE, PIECE), :]
    v_copies = [
        remote(
            v_send.at[rows_at(z_peer(d) * PIECE, PIECE)], v_recv.at[z], v_ssem.at[d], v_rsem.at[d], at_z(d)
        )
        for d in range(1, NZ)
    ]
    for copy in z_copies:
        copy.wait_recv()
    slots = [st_z[i] for i in range(NZ)]
    peak, total, sum_x, sum_y = merge(slots)
    mean_x, mean_y = sum_x / total, sum_y / total
    weight = SCALE / total
    coef[qry] = jnp.concatenate(
        [peak, grad_x * weight, mean_x, grad_y * weight, mean_y, zeros[0:3]], axis=0
    )
    st_loc[2] = coef[qry]
    c_copies = [
        remote(st_loc.at[2], coef.at[qry], c_send.at[d], c_recv.at[d], at_g(d)) for d in range(1, NG)
    ]

    def target_block(p, block, first):
        rows = coef[p]
        top, a_x, m_x, a_y, m_y = (rows[i : i + 1] for i in range(5))
        for r in range(OWN_T // FRAME_W):
            coord_y = row_coord(tgt * ROWS + qry * (OWN_T // FRAME_W) + r)
            offset = a_y * (coord_y - m_y)
            for k in range(0, FRAME_W, SUB):
                here = r * FRAME_W + k
                part = rows_at(qry * OWN_T + here, SUB)
                expo = jnp.exp2(scores_of(t_ref[part, :], block) * LOG2 - top)
                inner = (twice(cx_ref[k : k + SUB, :]) - m_x) * a_x + offset
                add = jnp.dot((expo * inner).astype(BF16), block, preferred_element_type=F32)
                out = pl.ds(here, SUB)
                if first:
                    gt_acc[out, :] = add
                else:
                    gt_acc[out, :] = gt_acc[out, :] + add

    target_block(qry, queries, True)

    for copy in v_copies:
        copy.wait_recv()
    piece = jnp.zeros((PIECE, NQ), F32)
    for i in range(NZ):
        s = slots[i]
        shift = grad_x * (s[5:6] - mean_x) + grad_y * (s[6:7] - mean_y)
        got = v_recv[i].astype(F32)
        piece = piece + jnp.exp2(s[4:5] - peak) * (got[:, :NQ] + shift * got[:, NQ:])
    part_y[NY] = piece * weight
    part_y[y] = part_y[NY]
    p_copies = [
        remote(part_y.at[NY], part_y.at[y], p_send.at[d], p_recv.at[d], at_y(d)) for d in range(1, NY)
    ]

    f_copies = []
    for d in range(1, NG):
        q_copies[d - 1].wait_recv()
        c_copies[d - 1].wait_recv()
        p = g_peer(NG - d)
        target_block(p, q_all[p], False)
        if d == 3:
            for copy in p_copies:
                copy.wait_recv()
            whole = part_y[0]
            for i in range(1, NY):
                whole = whole + part_y[i]
            piece_z[NZ] = whole.astype(BF16)
            piece_z[z] = piece_z[NZ]
            f_copies = [
                remote(piece_z.at[NZ], piece_z.at[z], f_send.at[e], f_recv.at[e], at_z(e))
                for e in range(1, NZ)
            ]
    gt_ref[...] = gt_acc[...].astype(BF16)
    for copy in f_copies:
        copy.wait_recv()
    full = piece_z[0:NZ].reshape(CHANNELS, NQ).astype(F32)
    gq_ref[...] = full.T.astype(BF16)

    for copy in q_copies + y_copies + z_copies + v_copies + c_copies + p_copies + f_copies:
        copy.wait_send()


def body(query_feat, target_feat, flow_grad):
    vmem = pl.BlockSpec(memory_space=pltpu.VMEM)
    sems = pltpu.SemaphoreType.DMA
    return pl.pallas_call(
        kernel,
        name="matching_backward",
        out_shape=(
            jax.ShapeDtypeStruct((NQ, CHANNELS), BF16),
            jax.ShapeDtypeStruct((OWN_T, CHANNELS), BF16),
        ),
        in_specs=[vmem, pl.BlockSpec(memory_space=pl.ANY), vmem],
        out_specs=(vmem, vmem),
        scratch_shapes=[
            pltpu.VMEM((NT, CHANNELS), BF16),
            pltpu.VMEM((NT, NQ), F32),
            pltpu.VMEM((FRAME_W, 128), F32),
            pltpu.VMEM((NT // SUB, 8, NQ), F32),
            pltpu.VMEM((NG, NQ, CHANNELS), BF16),
            pltpu.VMEM((3, 8, NQ), F32),
            pltpu.VMEM((NY, 8, NQ), F32),
            pltpu.VMEM((NZ, 8, NQ), F32),
            pltpu.VMEM((NG, 8, NQ), F32),
            pltpu.VMEM((CHANNELS, 2 * NQ), BF16),
            pltpu.VMEM((NZ, PIECE, 2 * NQ), BF16),
            pltpu.VMEM((NY + 1, PIECE, NQ), F32),
            pltpu.VMEM((NZ + 1, PIECE, NQ), BF16),
            pltpu.VMEM((OWN_T, CHANNELS), F32),
            sems((GROUPS,)),
            sems((NG,)), sems((NG,)),
            sems((NY,)), sems((NY,)),
            sems((NZ,)), sems((NZ,)),
            sems((NG,)), sems((NG,)),
            sems((NZ,)), sems((NZ,)),
            sems((NY,)), sems((NY,)),
            sems((NZ,)), sems((NZ,)),
        ],
        compiler_params=pltpu.CompilerParams(
            collective_id=0, has_side_effects=True, vmem_limit_bytes=56 * 2**20
        ),
    )(query_feat, target_feat, flow_grad)


def solution(mesh):
    placed = (P("qry", None), P("tgt", None), P("qry", None))
    return jax.shard_map(
        body,
        mesh=mesh,
        in_specs=placed,
        out_specs=(P("qry", None), P(("tgt", "qry"), None)),
        check_vma=False,
    )
```

```python
import math

import jax
import jax.numpy as jnp
from jax import lax
from jax.experimental import pallas as pl
from jax.experimental.pallas import tpu as pltpu
from jax.sharding import PartitionSpec as P

MESH = pl.DeviceIdType.MESH
F32, BF16 = jnp.float32, jnp.bfloat16

CHANNELS = 128
FRAME_W = 1024
NQ = 256
NT = 16384
ROWS = NT // FRAME_W
OWN_T = 2048
NZ, NY, NG = 8, 4, 8
PIECE = CHANNELS // NZ
SUB = 256
TILES = SUB // 8
GROUPS = 4
SCALE = 1.0 / math.sqrt(CHANNELS)
LOG2 = SCALE * math.log2(math.e)


def twice(column):
    return jnp.concatenate([column, column], axis=1)


def scores_of(targets, queries):
    return lax.dot_general(targets, queries, (((1,), (1,)), ((), ())), preferred_element_type=F32)


def row_coord(row):
    return (2.0 * row.astype(F32) + 1.0) / FRAME_W - 1.0


def rows_at(start, count):
    return pl.ds(pl.multiple_of(start, count), count)


def kernel(
    q_ref, t_hbm, g_ref, gq_ref, gt_ref,
    t_ref, e_ref, cx_ref, xt_ref, peak_ref, top_ref, q_all, st_loc, st_y, st_z, coef, v_send, v_recv,
    part_y, piece_z,
    t_sem, q_send, q_recv, y_send, y_recv, z_send, z_recv, c_send, c_recv,
    v_ssem, v_rsem, p_send, p_recv, f_send, f_recv,
):
    tgt, qry = lax.axis_index("tgt"), lax.axis_index("qry")
    z, y = tgt // NY, lax.rem(tgt, NY)

    def z_peer(d):
        return lax.rem(z + d, NZ)

    def y_peer(d):
        return lax.rem(y + d, NY)

    def g_peer(d):
        return lax.rem(qry + d, NG)

    def at_z(d):
        return (z_peer(d) * NY + y, qry)

    def at_y(d):
        return (z * NY + y_peer(d), qry)

    def at_g(d):
        return (tgt, g_peer(d))

    barrier = pltpu.get_barrier_semaphore()
    for d in range(1, NY):
        pl.semaphore_signal(barrier, inc=1, device_id=at_y(d), device_id_type=MESH)
    for d in range(1, NG):
        pl.semaphore_signal(barrier, inc=1, device_id=at_g(d), device_id_type=MESH)
    for d in range(1, NZ):
        pl.semaphore_signal(barrier, inc=1, device_id=at_z(d), device_id_type=MESH)

    def load(i):
        part = rows_at(i * (NT // GROUPS), NT // GROUPS)
        return pltpu.make_async_copy(t_hbm.at[part], t_ref.at[part], t_sem.at[i])

    for i in range(GROUPS):
        load(i).start()

    def remote(src, dst, ssem, rsem, where):
        copy = pltpu.make_async_remote_copy(
            src_ref=src, dst_ref=dst, send_sem=ssem, recv_sem=rsem, device_id=where, device_id_type=MESH
        )
        copy.start()
        return copy

    column = lax.broadcasted_iota(jnp.int32, (FRAME_W, 128), 0)
    cx_ref[...] = row_coord(column)
    queries = q_ref[...]
    grads = g_ref[...].astype(F32)
    grad_x, grad_y = grads[0:1], grads[1:2]

    def stats_row(b, carry):
        peak, total, sum_x, sum_y = carry
        coord_y = row_coord(tgt * ROWS + b)
        for k in range(0, FRAME_W, SUB):
            part = rows_at(b * FRAME_W + k, SUB)
            scores = scores_of(t_ref[part, :], queries).reshape(TILES, 8, NQ)
            top = jnp.maximum(peak, jnp.max(scores, axis=0) * LOG2)
            factor = jnp.exp2(peak - top)
            expo = jnp.exp2(scores * LOG2 - top[None])
            tot = expo[0]
            ahead = tot
            for i in range(1, TILES):
                tot = tot + expo[i]
                ahead = ahead + tot
            x_part = twice(cx_ref[k : k + 8, :]) * tot + (TILES * tot - ahead) * (16.0 / FRAME_W)
            total = total * factor + tot
            sum_x = sum_x * factor + x_part
            sum_y = sum_y * factor + coord_y * tot
            peak = top
            e_ref[part, :] = expo.reshape(SUB, NQ)
            peak_ref[b * (FRAME_W // SUB) + k // SUB] = top
        return peak, total, sum_x, sum_y

    def stats_group(i, carry):
        load(i).wait()
        for r in range(ROWS // GROUPS):
            carry = stats_row(i * (ROWS // GROUPS) + r, carry)
        return carry

    zeros = jnp.zeros((8, NQ), F32)
    carry = (jnp.full((8, NQ), -1e30, F32), zeros, zeros, zeros)
    carry = lax.fori_loop(0, GROUPS - 1, stats_group, carry)

    pl.semaphore_wait(barrier, NY - 1 + NG - 1 + NZ - 1)
    q_copies = [
        remote(q_ref, q_all.at[qry], q_send.at[d], q_recv.at[d], at_g(d)) for d in range(1, NG)
    ]

    carry = lax.fori_loop(GROUPS - 1, GROUPS, stats_group, carry)

    peak8, total8, x8, y8 = carry
    peak_l = jnp.max(peak8, axis=0, keepdims=True)
    factor8 = jnp.exp2(peak8 - peak_l)
    total_l = jnp.sum(total8 * factor8, axis=0, keepdims=True)
    sum_xl = jnp.sum(x8 * factor8, axis=0, keepdims=True)
    sum_yl = jnp.sum(y8 * factor8, axis=0, keepdims=True)
    mean_xl, mean_yl = sum_xl / total_l, sum_yl / total_l

    st_loc[0] = jnp.concatenate([peak_l, total_l, sum_xl, sum_yl, zeros[0:4]], axis=0)
    st_y[y] = st_loc[0]
    y_copies = [
        remote(st_loc.at[0], st_y.at[y], y_send.at[d], y_recv.at[d], at_y(d)) for d in range(1, NY)
    ]

    xt_ref[...] = (twice(cx_ref[...]) - mean_xl) * grad_x

    def grad_row(b, acc):
        coord_y = row_coord(tgt * ROWS + b)
        offset = grad_y * (coord_y - mean_yl)
        parts = []
        for k in range(0, FRAME_W, SUB):
            part = rows_at(b * FRAME_W + k, SUB)
            factor = jnp.exp2(peak_ref[b * (FRAME_W // SUB) + k // SUB] - peak_l)
            expo = (e_ref[part, :].reshape(TILES, 8, NQ) * factor[None]).reshape(SUB, NQ)
            inner = xt_ref[k : k + SUB, :] + offset
            parts.append(jnp.concatenate([(expo * inner).astype(BF16), expo.astype(BF16)], axis=1))
        block = t_ref[rows_at(b * FRAME_W, FRAME_W), :]
        return acc + lax.dot_general(
            block, jnp.concatenate(parts, axis=0), (((0,), (0,)), ((), ())), preferred_element_type=F32
        )

    def grad_group(i, acc):
        for r in range(ROWS // GROUPS):
            acc = grad_row(i * (ROWS // GROUPS) + r, acc)
        return acc

    v = lax.fori_loop(0, GROUPS, grad_group, jnp.zeros((CHANNELS, 2 * NQ), F32))

    def merge(slots):
        peak = slots[0][0:1]
        for s in slots[1:]:
            peak = jnp.maximum(peak, s[0:1])
        total = sum_x = sum_y = jnp.zeros((1, NQ), F32)
        for s in slots:
            factor = jnp.exp2(s[0:1] - peak)
            total = total + s[1:2] * factor
            sum_x = sum_x + s[2:3] * factor
            sum_y = sum_y + s[3:4] * factor
        return peak, total, sum_x, sum_y

    for copy in y_copies:
        copy.wait_recv()
    merged = merge([st_y[i] for i in range(NY)])
    st_loc[1] = jnp.concatenate([*merged, peak_l, mean_xl, mean_yl, zeros[0:1]], axis=0)
    st_z[z] = st_loc[1]
    z_copies = [
        remote(st_loc.at[1], st_z.at[z], z_send.at[d], z_recv.at[d], at_z(d)) for d in range(1, NZ)
    ]
    v_send[...] = v.astype(BF16)
    v_recv[z] = v_send[rows_at(z * PIECE, PIECE), :]
    v_copies = [
        remote(
            v_send.at[rows_at(z_peer(d) * PIECE, PIECE)], v_recv.at[z], v_ssem.at[d], v_rsem.at[d], at_z(d)
        )
        for d in range(1, NZ)
    ]
    def target_expo(d, block):
        for k in range(0, OWN_T, SUB):
            scores = scores_of(t_ref[rows_at(qry * OWN_T + k, SUB), :], block).reshape(TILES, 8, NQ)
            top = jnp.max(scores, axis=0) * LOG2
            expo = jnp.exp2(scores * LOG2 - top[None])
            e_ref[d * OWN_T + k : d * OWN_T + k + SUB, :] = expo.reshape(SUB, NQ)
            top_ref[(d * OWN_T + k) // SUB] = top

    target_expo(0, queries)
    for d in range(1, NG):
        q_copies[d - 1].wait_recv()
        target_expo(d, q_all[g_peer(NG - d)])

    for copy in z_copies:
        copy.wait_recv()
    slots = [st_z[i] for i in range(NZ)]
    peak, total, sum_x, sum_y = merge(slots)
    mean_x, mean_y = sum_x / total, sum_y / total
    weight = SCALE / total
    coef[qry] = jnp.concatenate(
        [peak, grad_x * weight, mean_x, grad_y * weight, mean_y, zeros[0:3]], axis=0
    )
    st_loc[2] = coef[qry]
    c_copies = [
        remote(st_loc.at[2], coef.at[qry], c_send.at[d], c_recv.at[d], at_g(d)) for d in range(1, NG)
    ]

    def target_block(d, p, block):
        rows = coef[p]
        top, a_x, m_x, a_y, m_y = (rows[i : i + 1] for i in range(5))
        for r in range(OWN_T // FRAME_W):
            coord_y = row_coord(tgt * ROWS + qry * (OWN_T // FRAME_W) + r)
            shift = a_y * (coord_y - m_y)
            for k in range(0, FRAME_W, SUB):
                here = r * FRAME_W + k
                factor = jnp.exp2(top_ref[(d * OWN_T + here) // SUB] - top)
                slope, offset = (factor * a_x)[None], (factor * shift)[None]
                expo = e_ref[d * OWN_T + here : d * OWN_T + here + SUB, :].reshape(TILES, 8, NQ)
                away = (twice(cx_ref[k : k + SUB, :]) - m_x).reshape(TILES, 8, NQ)
                dscore = (expo * (away * slope + offset)).reshape(SUB, NQ).astype(BF16)
                add = jnp.dot(dscore, block, preferred_element_type=F32)
                out = pl.ds(here, SUB)
                gt_ref[out, :] = add if d == 0 else gt_ref[out, :] + add

    target_block(0, qry, queries)

    for copy in v_copies:
        copy.wait_recv()
    piece = jnp.zeros((PIECE, NQ), F32)
    for i in range(NZ):
        s = slots[i]
        shift = grad_x * (s[5:6] - mean_x) + grad_y * (s[6:7] - mean_y)
        got = v_recv[i].astype(F32)
        piece = piece + jnp.exp2(s[4:5] - peak) * (got[:, :NQ] + shift * got[:, NQ:])
    part_y[NY] = piece * weight
    part_y[y] = part_y[NY]
    p_copies = [
        remote(part_y.at[NY], part_y.at[y], p_send.at[d], p_recv.at[d], at_y(d)) for d in range(1, NY)
    ]

    f_copies = []
    for d in range(1, NG):
        c_copies[d - 1].wait_recv()
        p = g_peer(NG - d)
        target_block(d, p, q_all[p])
        if d == 2:
            for copy in p_copies:
                copy.wait_recv()
            whole = part_y[0]
            for i in range(1, NY):
                whole = whole + part_y[i]
            piece_z[NZ] = whole.astype(BF16)
            piece_z[z] = piece_z[NZ]
            f_copies = [
                remote(piece_z.at[NZ], piece_z.at[z], f_send.at[e], f_recv.at[e], at_z(e))
                for e in range(1, NZ)
            ]
    for copy in f_copies:
        copy.wait_recv()
    full = piece_z[0:NZ].reshape(CHANNELS, NQ).astype(F32)
    gq_ref[...] = full.T

    for copy in q_copies + y_copies + z_copies + v_copies + c_copies + p_copies + f_copies:
        copy.wait_send()


def body(query_feat, target_feat, flow_grad):
    vmem = pl.BlockSpec(memory_space=pltpu.VMEM)
    sems = pltpu.SemaphoreType.DMA
    grad_query, grad_target = pl.pallas_call(
        kernel,
        name="matching_backward",
        out_shape=(
            jax.ShapeDtypeStruct((NQ, CHANNELS), F32),
            jax.ShapeDtypeStruct((OWN_T, CHANNELS), F32),
        ),
        in_specs=[vmem, pl.BlockSpec(memory_space=pl.ANY), vmem],
        out_specs=(vmem, vmem),
        scratch_shapes=[
            pltpu.VMEM((NT, CHANNELS), BF16),
            pltpu.VMEM((NT, NQ), F32),
            pltpu.VMEM((FRAME_W, 128), F32),
            pltpu.VMEM((FRAME_W, NQ), F32),
            pltpu.VMEM((NT // SUB, 8, NQ), F32),
            pltpu.VMEM((NG * OWN_T // SUB, 8, NQ), F32),
            pltpu.VMEM((NG, NQ, CHANNELS), BF16),
            pltpu.VMEM((3, 8, NQ), F32),
            pltpu.VMEM((NY, 8, NQ), F32),
            pltpu.VMEM((NZ, 8, NQ), F32),
            pltpu.VMEM((NG, 8, NQ), F32),
            pltpu.VMEM((CHANNELS, 2 * NQ), BF16),
            pltpu.VMEM((NZ, PIECE, 2 * NQ), BF16),
            pltpu.VMEM((NY + 1, PIECE, NQ), F32),
            pltpu.VMEM((NZ + 1, PIECE, NQ), BF16),
            sems((GROUPS,)),
            sems((NG,)), sems((NG,)),
            sems((NY,)), sems((NY,)),
            sems((NZ,)), sems((NZ,)),
            sems((NG,)), sems((NG,)),
            sems((NZ,)), sems((NZ,)),
            sems((NY,)), sems((NY,)),
            sems((NZ,)), sems((NZ,)),
        ],
        compiler_params=pltpu.CompilerParams(
            collective_id=0, has_side_effects=True, vmem_limit_bytes=56 * 2**20
        ),
    )(query_feat, target_feat, flow_grad.T)
    return grad_query.astype(BF16), grad_target.astype(BF16)


def solution(mesh):
    placed = (P("qry", None), P("tgt", None), P("qry", None))
    return jax.shard_map(
        body,
        mesh=mesh,
        in_specs=placed,
        out_specs=(P("qry", None), P(("tgt", "qry"), None)),
        check_vma=False,
    )
```

```python
import math

import jax
import jax.numpy as jnp
from jax import lax
from jax.experimental import pallas as pl
from jax.experimental.pallas import tpu as pltpu
from jax.sharding import PartitionSpec as P

MESH = pl.DeviceIdType.MESH
F32, BF16 = jnp.float32, jnp.bfloat16

CHANNELS = 128
FRAME_W = 1024
NQ = 256
NT = 16384
ROWS = NT // FRAME_W
OWN_T = 2048
NZ, NY, NG = 8, 4, 8
PIECE = CHANNELS // NZ
SUB = 256
TILES = SUB // 8
CUTS = 4
GROUPS = 4
SCALE = 1.0 / math.sqrt(CHANNELS)
LOG2 = SCALE * math.log2(math.e)


def twice(column):
    return jnp.concatenate([column, column], axis=1)


def scores_of(targets, queries):
    return lax.dot_general(targets, queries, (((1,), (1,)), ((), ())), preferred_element_type=F32)


def row_coord(row):
    return (2.0 * row.astype(F32) + 1.0) / FRAME_W - 1.0


def rows_at(start, count):
    return pl.ds(pl.multiple_of(start, count), count)


def kernel(
    q_ref, t_hbm, g_ref, gq_ref, gt_ref,
    t_ref, e_ref, cx_ref, xt_ref, peak_ref, top_ref, q_all, st_loc, st_y, st_z, coef, v_send, v_recv,
    part_y, piece_z, gt_acc, gt_out,
    t_sem, o_sem, q_send, q_recv, y_send, y_recv, z_send, z_recv, c_send, c_recv,
    v_ssem, v_rsem, p_send, p_recv, f_send, f_recv,
):
    tgt, qry = lax.axis_index("tgt"), lax.axis_index("qry")
    z, y = tgt // NY, lax.rem(tgt, NY)

    def z_peer(d):
        return lax.rem(z + d, NZ)

    def y_peer(d):
        return lax.rem(y + d, NY)

    def g_peer(d):
        return lax.rem(qry + d, NG)

    def at_z(d):
        return (z_peer(d) * NY + y, qry)

    def at_y(d):
        return (z * NY + y_peer(d), qry)

    def at_g(d):
        return (tgt, g_peer(d))

    barrier = pltpu.get_barrier_semaphore()
    for d in range(1, NY):
        pl.semaphore_signal(barrier, inc=1, device_id=at_y(d), device_id_type=MESH)
    for d in range(1, NG):
        pl.semaphore_signal(barrier, inc=1, device_id=at_g(d), device_id_type=MESH)
    for d in range(1, NZ):
        pl.semaphore_signal(barrier, inc=1, device_id=at_z(d), device_id_type=MESH)

    def load(i):
        part = rows_at(i * (NT // GROUPS), NT // GROUPS)
        return pltpu.make_async_copy(t_hbm.at[part], t_ref.at[part], t_sem.at[i])

    for i in range(GROUPS):
        load(i).start()

    def store(i):
        part = pl.ds(i * FRAME_W, FRAME_W)
        return pltpu.make_async_copy(gt_out.at[part], gt_ref.at[part], o_sem.at[i])

    def remote(src, dst, ssem, rsem, where):
        copy = pltpu.make_async_remote_copy(
            src_ref=src, dst_ref=dst, send_sem=ssem, recv_sem=rsem, device_id=where, device_id_type=MESH
        )
        copy.start()
        return copy

    column = lax.broadcasted_iota(jnp.int32, (FRAME_W, 128), 0)
    cx_ref[...] = row_coord(column)
    queries = q_ref[...]
    grads = g_ref[...].astype(F32)
    grad_x, grad_y = grads[0:1], grads[1:2]

    def stats_row(b, carry):
        peak, total, sum_x, sum_y = carry
        coord_y = row_coord(tgt * ROWS + b)
        for k in range(0, FRAME_W, SUB):
            part = rows_at(b * FRAME_W + k, SUB)
            scores = scores_of(t_ref[part, :], queries).reshape(TILES, 8, NQ)
            top = jnp.maximum(peak, jnp.max(scores, axis=0) * LOG2)
            factor = jnp.exp2(peak - top)
            expo = jnp.exp2(scores * LOG2 - top[None])
            tot = expo[0]
            ahead = tot
            for i in range(1, TILES):
                tot = tot + expo[i]
                ahead = ahead + tot
            x_part = twice(cx_ref[k : k + 8, :]) * tot + (TILES * tot - ahead) * (16.0 / FRAME_W)
            total = total * factor + tot
            sum_x = sum_x * factor + x_part
            sum_y = sum_y * factor + coord_y * tot
            peak = top
            e_ref[part, :] = expo.reshape(SUB, NQ)
            peak_ref[b * (FRAME_W // SUB) + k // SUB] = top
        return peak, total, sum_x, sum_y

    def stats_group(i, carry):
        load(i).wait()
        for r in range(ROWS // GROUPS):
            carry = stats_row(i * (ROWS // GROUPS) + r, carry)
        return carry

    zeros = jnp.zeros((8, NQ), F32)
    carry = (jnp.full((8, NQ), -1e30, F32), zeros, zeros, zeros)
    carry = lax.fori_loop(0, GROUPS - 1, stats_group, carry)

    pl.semaphore_wait(barrier, NY - 1 + NG - 1 + NZ - 1)
    q_copies = [
        remote(q_ref, q_all.at[qry], q_send.at[d], q_recv.at[d], at_g(d)) for d in range(1, NG)
    ]

    carry = lax.fori_loop(GROUPS - 1, GROUPS, stats_group, carry)

    peak8, total8, x8, y8 = carry
    peak_l = jnp.max(peak8, axis=0, keepdims=True)
    factor8 = jnp.exp2(peak8 - peak_l)
    total_l = jnp.sum(total8 * factor8, axis=0, keepdims=True)
    sum_xl = jnp.sum(x8 * factor8, axis=0, keepdims=True)
    sum_yl = jnp.sum(y8 * factor8, axis=0, keepdims=True)
    mean_xl, mean_yl = sum_xl / total_l, sum_yl / total_l

    st_loc[0] = jnp.concatenate([peak_l, total_l, sum_xl, sum_yl, zeros[0:4]], axis=0)
    st_y[y] = st_loc[0]
    y_copies = [
        remote(st_loc.at[0], st_y.at[y], y_send.at[d], y_recv.at[d], at_y(d)) for d in range(1, NY)
    ]

    xt_ref[...] = (twice(cx_ref[...]) - mean_xl) * grad_x

    def grad_row(b, acc):
        coord_y = row_coord(tgt * ROWS + b)
        offset = grad_y * (coord_y - mean_yl)
        parts = []
        for k in range(0, FRAME_W, SUB):
            part = rows_at(b * FRAME_W + k, SUB)
            factor = jnp.exp2(peak_ref[b * (FRAME_W // SUB) + k // SUB] - peak_l)
            expo = (e_ref[part, :].reshape(TILES, 8, NQ) * factor[None]).reshape(SUB, NQ)
            inner = xt_ref[k : k + SUB, :] + offset
            parts.append(jnp.concatenate([(expo * inner).astype(BF16), expo.astype(BF16)], axis=1))
        block = t_ref[rows_at(b * FRAME_W, FRAME_W), :]
        return acc + lax.dot_general(
            block, jnp.concatenate(parts, axis=0), (((0,), (0,)), ((), ())), preferred_element_type=F32
        )

    def grad_group(i, acc):
        for r in range(ROWS // GROUPS):
            acc = grad_row(i * (ROWS // GROUPS) + r, acc)
        return acc

    v = lax.fori_loop(0, GROUPS, grad_group, jnp.zeros((CHANNELS, 2 * NQ), F32))

    def merge(slots):
        peak = slots[0][0:1]
        for s in slots[1:]:
            peak = jnp.maximum(peak, s[0:1])
        total = sum_x = sum_y = jnp.zeros((1, NQ), F32)
        for s in slots:
            factor = jnp.exp2(s[0:1] - peak)
            total = total + s[1:2] * factor
            sum_x = sum_x + s[2:3] * factor
            sum_y = sum_y + s[3:4] * factor
        return peak, total, sum_x, sum_y

    for copy in y_copies:
        copy.wait_recv()
    merged = merge([st_y[i] for i in range(NY)])
    st_loc[1] = jnp.concatenate([*merged, peak_l, mean_xl, mean_yl, zeros[0:1]], axis=0)
    st_z[z] = st_loc[1]
    z_copies = [
        remote(st_loc.at[1], st_z.at[z], z_send.at[d], z_recv.at[d], at_z(d)) for d in range(1, NZ)
    ]
    v_send[...] = v.astype(BF16)
    v_recv[z] = v_send[rows_at(z * PIECE, PIECE), :]
    v_copies = [
        remote(
            v_send.at[rows_at(z_peer(d) * PIECE, PIECE)], v_recv.at[z], v_ssem.at[d], v_rsem.at[d], at_z(d)
        )
        for d in range(1, NZ)
    ]
    def target_expo(d, block):
        for k in range(0, OWN_T, SUB):
            scores = scores_of(t_ref[rows_at(qry * OWN_T + k, SUB), :], block).reshape(TILES, 8, NQ)
            top = jnp.max(scores, axis=0) * LOG2
            expo = jnp.exp2(scores * LOG2 - top[None])
            e_ref[d * OWN_T + k : d * OWN_T + k + SUB, :] = expo.reshape(SUB, NQ)
            top_ref[(d * OWN_T + k) // SUB] = top

    target_expo(0, queries)
    for d in range(1, NG):
        q_copies[d - 1].wait_recv()
        target_expo(d, q_all[g_peer(NG - d)])

    for copy in z_copies:
        copy.wait_recv()
    slots = [st_z[i] for i in range(NZ)]
    peak, total, sum_x, sum_y = merge(slots)
    mean_x, mean_y = sum_x / total, sum_y / total
    weight = SCALE / total
    coef[qry] = jnp.concatenate(
        [peak, grad_x * weight, mean_x, grad_y * weight, mean_y, zeros[0:3]], axis=0
    )
    st_loc[2] = coef[qry]
    c_copies = [
        remote(st_loc.at[2], coef.at[qry], c_send.at[d], c_recv.at[d], at_g(d)) for d in range(1, NG)
    ]

    def target_block(d, p, block):
        rows = coef[p]
        top, a_x, m_x, a_y, m_y = (rows[i : i + 1] for i in range(5))
        for r in range(OWN_T // FRAME_W):
            coord_y = row_coord(tgt * ROWS + qry * (OWN_T // FRAME_W) + r)
            shift = a_y * (coord_y - m_y)
            for k in range(0, FRAME_W, SUB):
                here = r * FRAME_W + k
                factor = jnp.exp2(top_ref[(d * OWN_T + here) // SUB] - top)
                slope, offset = (factor * a_x)[None], (factor * shift)[None]
                expo = e_ref[d * OWN_T + here : d * OWN_T + here + SUB, :].reshape(TILES, 8, NQ)
                away = (twice(cx_ref[k : k + SUB, :]) - m_x).reshape(TILES, 8, NQ)
                dscore = (expo * (away * slope + offset)).reshape(SUB, NQ).astype(BF16)
                add = jnp.dot(dscore, block, preferred_element_type=F32)
                out = pl.ds(here, SUB)
                if d == NG - 1:
                    gt_out[out, :] = (gt_acc[out, :] + add).astype(BF16)
                else:
                    gt_acc[out, :] = add if d == 0 else gt_acc[out, :] + add
            if d == NG - 1:
                store(r).start()

    for copy in v_copies:
        copy.wait_recv()
    piece = jnp.zeros((PIECE, NQ), F32)
    for i in range(NZ):
        s = slots[i]
        shift = grad_x * (s[5:6] - mean_x) + grad_y * (s[6:7] - mean_y)
        got = v_recv[i].astype(F32)
        piece = piece + jnp.exp2(s[4:5] - peak) * (got[:, :NQ] + shift * got[:, NQ:])
    part_y[NY] = piece * weight
    part_y[y] = part_y[NY]
    p_copies = [
        remote(part_y.at[NY], part_y.at[y], p_send.at[d], p_recv.at[d], at_y(d)) for d in range(1, NY)
    ]

    target_block(0, qry, queries)
    f_copies = []
    for d in range(1, NG):
        c_copies[d - 1].wait_recv()
        p = g_peer(NG - d)
        target_block(d, p, q_all[p])
        if d == 2:
            for copy in p_copies:
                copy.wait_recv()
            whole = part_y[0]
            for i in range(1, NY):
                whole = whole + part_y[i]
            piece_z[NZ] = whole.astype(BF16)
            piece_z[z] = piece_z[NZ]
            f_copies = [
                remote(piece_z.at[NZ], piece_z.at[z], f_send.at[e], f_recv.at[e], at_z(e))
                for e in range(1, NZ)
            ]
    for copy in f_copies:
        copy.wait_recv()
    full = piece_z[0:NZ].reshape(CHANNELS, NQ).astype(F32)
    gq_ref[...] = full.T.astype(BF16)
    for i in range(OWN_T // FRAME_W):
        store(i).wait()

    for copy in q_copies + y_copies + z_copies + v_copies + c_copies + p_copies + f_copies:
        copy.wait_send()


def copy_kernel(gq_in, gt_in, gq_out, gt_out, gq_v, gt_v, sem):
    parts = [(gq_in, gq_v, gq_out)]
    for i in range(CUTS):
        part = pl.ds(i * (OWN_T // CUTS), OWN_T // CUTS)
        parts.append((gt_in.at[part], gt_v.at[part], gt_out.at[part]))
    into = [pltpu.make_async_copy(a, b, sem.at[0, i]) for i, (a, b, _) in enumerate(parts)]
    out = [pltpu.make_async_copy(b, c, sem.at[1, i]) for i, (_, b, c) in enumerate(parts)]
    for copy in into:
        copy.start()
    for first, second in zip(into, out):
        first.wait()
        second.start()
    for copy in out:
        copy.wait()


def hand_over(grad_query, grad_target):
    anywhere = pl.BlockSpec(memory_space=pl.ANY)
    shapes = [jax.ShapeDtypeStruct(a.shape, a.dtype) for a in (grad_query, grad_target)]
    return pl.pallas_call(
        copy_kernel,
        name="hand_over",
        out_shape=tuple(shapes),
        in_specs=[anywhere, anywhere],
        out_specs=(anywhere, anywhere),
        scratch_shapes=[
            *(pltpu.VMEM(s.shape, s.dtype) for s in shapes),
            pltpu.SemaphoreType.DMA((2, CUTS + 1)),
        ],
        compiler_params=pltpu.CompilerParams(vmem_limit_bytes=60 * 2**20),
    )(grad_query, grad_target)


def body(query_feat, target_feat, flow_grad):
    vmem = pl.BlockSpec(memory_space=pltpu.VMEM)
    sems = pltpu.SemaphoreType.DMA
    grad_query, grad_target = pl.pallas_call(
        kernel,
        name="matching_backward",
        out_shape=(
            jax.ShapeDtypeStruct((NQ, CHANNELS), BF16),
            jax.ShapeDtypeStruct((OWN_T, CHANNELS), BF16),
        ),
        in_specs=[vmem, pl.BlockSpec(memory_space=pl.ANY), vmem],
        out_specs=(vmem, pl.BlockSpec(memory_space=pl.ANY)),
        scratch_shapes=[
            pltpu.VMEM((NT, CHANNELS), BF16),
            pltpu.VMEM((NT, NQ), F32),
            pltpu.VMEM((FRAME_W, 128), F32),
            pltpu.VMEM((FRAME_W, NQ), F32),
            pltpu.VMEM((NT // SUB, 8, NQ), F32),
            pltpu.VMEM((NG * OWN_T // SUB, 8, NQ), F32),
            pltpu.VMEM((NG, NQ, CHANNELS), BF16),
            pltpu.VMEM((3, 8, NQ), F32),
            pltpu.VMEM((NY, 8, NQ), F32),
            pltpu.VMEM((NZ, 8, NQ), F32),
            pltpu.VMEM((NG, 8, NQ), F32),
            pltpu.VMEM((CHANNELS, 2 * NQ), BF16),
            pltpu.VMEM((NZ, PIECE, 2 * NQ), BF16),
            pltpu.VMEM((NY + 1, PIECE, NQ), F32),
            pltpu.VMEM((NZ + 1, PIECE, NQ), BF16),
            pltpu.VMEM((OWN_T, CHANNELS), F32),
            pltpu.VMEM((OWN_T, CHANNELS), BF16),
            sems((GROUPS,)),
            sems((OWN_T // FRAME_W,)),
            sems((NG,)), sems((NG,)),
            sems((NY,)), sems((NY,)),
            sems((NZ,)), sems((NZ,)),
            sems((NG,)), sems((NG,)),
            sems((NZ,)), sems((NZ,)),
            sems((NY,)), sems((NY,)),
            sems((NZ,)), sems((NZ,)),
        ],
        compiler_params=pltpu.CompilerParams(
            collective_id=0, has_side_effects=True, vmem_limit_bytes=56 * 2**20
        ),
    )(query_feat, target_feat, flow_grad.T)
    return hand_over(grad_query, grad_target)


def solution(mesh):
    placed = (P("qry", None), P("tgt", None), P("qry", None))
    return jax.shard_map(
        body,
        mesh=mesh,
        in_specs=placed,
        out_specs=(P("qry", None), P(("tgt", "qry"), None)),
        check_vma=False,
    )
```

```python
import math

import jax
import jax.numpy as jnp
from jax import lax
from jax.experimental import pallas as pl
from jax.experimental.pallas import tpu as pltpu
from jax.sharding import PartitionSpec as P

MESH = pl.DeviceIdType.MESH
F32, BF16 = jnp.float32, jnp.bfloat16

CHANNELS = 128
FRAME_W = 1024
NQ = 256
NT = 16384
ROWS = NT // FRAME_W
OWN_T = 2048
NZ, NY, NG = 8, 4, 8
PIECE = CHANNELS // NZ
SUB = 256
TILES = SUB // 8
Z_ORDER = (4, 3, 5, 2, 6, 1, 7)
Y_ORDER = (2, 1, 3)
G_ORDER = (4, 3, 5, 2, 6, 1, 7)
EARLY = 3
GROUPS = 4
SCALE = 1.0 / math.sqrt(CHANNELS)
LOG2 = SCALE * math.log2(math.e)


def twice(column):
    return jnp.concatenate([column, column], axis=1)


def scores_of(targets, queries):
    return lax.dot_general(targets, queries, (((1,), (1,)), ((), ())), preferred_element_type=F32)


def row_coord(row):
    return (2.0 * row.astype(F32) + 1.0) / FRAME_W - 1.0


def rows_at(start, count):
    return pl.ds(pl.multiple_of(start, count), count)


def kernel(
    q_ref, t_hbm, g_ref, gq_ref, gt_ref,
    t_ref, e_ref, cx_ref, xt_ref, peak_ref, top_ref, q_all, st_loc, st_y, st_z, coef, v_send, v_recv,
    part_y, piece_z, gt_acc,
    t_sem, q_send, q_recv, y_send, y_recv, z_send, z_recv, c_send, c_recv,
    v_ssem, v_rsem, p_send, p_recv, f_send, f_recv,
):
    tgt, qry = lax.axis_index("tgt"), lax.axis_index("qry")
    z, y = tgt // NY, lax.rem(tgt, NY)

    def z_peer(d):
        return lax.rem(z + d, NZ)

    def y_peer(d):
        return lax.rem(y + d, NY)

    def g_peer(d):
        return lax.rem(qry + d, NG)

    def at_z(d):
        return (z_peer(d) * NY + y, qry)

    def at_y(d):
        return (z * NY + y_peer(d), qry)

    def at_g(d):
        return (tgt, g_peer(d))

    barrier = pltpu.get_barrier_semaphore()
    for d in range(1, NY):
        pl.semaphore_signal(barrier, inc=1, device_id=at_y(d), device_id_type=MESH)
    for d in range(1, NG):
        pl.semaphore_signal(barrier, inc=1, device_id=at_g(d), device_id_type=MESH)
    for d in range(1, NZ):
        pl.semaphore_signal(barrier, inc=1, device_id=at_z(d), device_id_type=MESH)

    def load(i):
        part = rows_at(i * (NT // GROUPS), NT // GROUPS)
        return pltpu.make_async_copy(t_hbm.at[part], t_ref.at[part], t_sem.at[i])

    for i in range(GROUPS):
        load(i).start()

    def remote(src, dst, ssem, rsem, where):
        copy = pltpu.make_async_remote_copy(
            src_ref=src, dst_ref=dst, send_sem=ssem, recv_sem=rsem, device_id=where, device_id_type=MESH
        )
        copy.start()
        return copy

    column = lax.broadcasted_iota(jnp.int32, (FRAME_W, 128), 0)
    cx_ref[...] = row_coord(column)
    queries = q_ref[...]
    grads = g_ref[...].astype(F32)
    grad_x, grad_y = grads[0:1], grads[1:2]

    def stats_row(b, carry):
        peak, total, sum_x, sum_y = carry
        coord_y = row_coord(tgt * ROWS + b)
        for k in range(0, FRAME_W, SUB):
            part = rows_at(b * FRAME_W + k, SUB)
            scores = scores_of(t_ref[part, :], queries).reshape(TILES, 8, NQ)
            top = jnp.maximum(peak, jnp.max(scores, axis=0) * LOG2)
            factor = jnp.exp2(peak - top)
            expo = jnp.exp2(scores * LOG2 - top[None])
            tot = expo[0]
            ahead = tot
            for i in range(1, TILES):
                tot = tot + expo[i]
                ahead = ahead + tot
            x_part = twice(cx_ref[k : k + 8, :]) * tot + (TILES * tot - ahead) * (16.0 / FRAME_W)
            total = total * factor + tot
            sum_x = sum_x * factor + x_part
            sum_y = sum_y * factor + coord_y * tot
            peak = top
            e_ref[part, :] = expo.reshape(SUB, NQ)
            peak_ref[b * (FRAME_W // SUB) + k // SUB] = top
        return peak, total, sum_x, sum_y

    def stats_group(i, carry):
        load(i).wait()
        for r in range(ROWS // GROUPS):
            carry = stats_row(i * (ROWS // GROUPS) + r, carry)
        return carry

    zeros = jnp.zeros((8, NQ), F32)
    carry = (jnp.full((8, NQ), -1e30, F32), zeros, zeros, zeros)
    carry = lax.fori_loop(0, GROUPS - 1, stats_group, carry)

    pl.semaphore_wait(barrier, NY - 1 + NG - 1 + NZ - 1)
    q_copies = [
        remote(q_ref, q_all.at[qry], q_send.at[d], q_recv.at[d], at_g(d)) for d in G_ORDER
    ]

    carry = lax.fori_loop(GROUPS - 1, GROUPS, stats_group, carry)

    peak8, total8, x8, y8 = carry
    peak_l = jnp.max(peak8, axis=0, keepdims=True)
    factor8 = jnp.exp2(peak8 - peak_l)
    total_l = jnp.sum(total8 * factor8, axis=0, keepdims=True)
    sum_xl = jnp.sum(x8 * factor8, axis=0, keepdims=True)
    sum_yl = jnp.sum(y8 * factor8, axis=0, keepdims=True)
    mean_xl, mean_yl = sum_xl / total_l, sum_yl / total_l

    st_loc[0] = jnp.concatenate([peak_l, total_l, sum_xl, sum_yl, zeros[0:4]], axis=0)
    st_y[y] = st_loc[0]
    y_copies = [
        remote(st_loc.at[0], st_y.at[y], y_send.at[d], y_recv.at[d], at_y(d)) for d in Y_ORDER
    ]

    xt_ref[...] = (twice(cx_ref[...]) - mean_xl) * grad_x

    def grad_row(b, acc):
        coord_y = row_coord(tgt * ROWS + b)
        offset = grad_y * (coord_y - mean_yl)
        parts = []
        for k in range(0, FRAME_W, SUB):
            part = rows_at(b * FRAME_W + k, SUB)
            factor = jnp.exp2(peak_ref[b * (FRAME_W // SUB) + k // SUB] - peak_l)
            expo = (e_ref[part, :].reshape(TILES, 8, NQ) * factor[None]).reshape(SUB, NQ)
            inner = xt_ref[k : k + SUB, :] + offset
            parts.append(jnp.concatenate([(expo * inner).astype(BF16), expo.astype(BF16)], axis=1))
        block = t_ref[rows_at(b * FRAME_W, FRAME_W), :]
        return acc + lax.dot_general(
            block, jnp.concatenate(parts, axis=0), (((0,), (0,)), ((), ())), preferred_element_type=F32
        )

    def grad_group(i, acc):
        for r in range(ROWS // GROUPS):
            acc = grad_row(i * (ROWS // GROUPS) + r, acc)
        return acc

    v = lax.fori_loop(0, GROUPS, grad_group, jnp.zeros((CHANNELS, 2 * NQ), F32))

    def merge(slots):
        peak = slots[0][0:1]
        for s in slots[1:]:
            peak = jnp.maximum(peak, s[0:1])
        total = sum_x = sum_y = jnp.zeros((1, NQ), F32)
        for s in slots:
            factor = jnp.exp2(s[0:1] - peak)
            total = total + s[1:2] * factor
            sum_x = sum_x + s[2:3] * factor
            sum_y = sum_y + s[3:4] * factor
        return peak, total, sum_x, sum_y

    for copy in y_copies:
        copy.wait_recv()
    merged = merge([st_y[i] for i in range(NY)])
    st_loc[1] = jnp.concatenate([*merged, peak_l, mean_xl, mean_yl, zeros[0:1]], axis=0)
    st_z[z] = st_loc[1]
    z_copies = [
        remote(st_loc.at[1], st_z.at[z], z_send.at[d], z_recv.at[d], at_z(d)) for d in Z_ORDER
    ]
    v_send[...] = v.astype(BF16)
    v_recv[z] = v_send[rows_at(z * PIECE, PIECE), :]
    v_copies = [
        remote(
            v_send.at[rows_at(z_peer(d) * PIECE, PIECE)], v_recv.at[z], v_ssem.at[d], v_rsem.at[d], at_z(d)
        )
        for d in Z_ORDER
    ]
    def target_expo(d, block):
        for k in range(0, OWN_T, SUB):
            scores = scores_of(t_ref[rows_at(qry * OWN_T + k, SUB), :], block).reshape(TILES, 8, NQ)
            top = jnp.max(scores, axis=0) * LOG2
            expo = jnp.exp2(scores * LOG2 - top[None])
            e_ref[d * OWN_T + k : d * OWN_T + k + SUB, :] = expo.reshape(SUB, NQ)
            top_ref[(d * OWN_T + k) // SUB] = top

    def more_expo(first, last):
        for i in range(first, last):
            q_copies[i].wait_recv()
            target_expo(i + 1, q_all[g_peer(NG - G_ORDER[i])])

    target_expo(0, queries)
    more_expo(0, EARLY)

    for copy in z_copies:
        copy.wait_recv()
    slots = [st_z[i] for i in range(NZ)]
    peak, total, sum_x, sum_y = merge(slots)
    mean_x, mean_y = sum_x / total, sum_y / total
    weight = SCALE / total
    coef[qry] = jnp.concatenate(
        [peak, grad_x * weight, mean_x, grad_y * weight, mean_y, zeros[0:3]], axis=0
    )
    def target_block(d, p, block):
        rows = coef[p]
        top, a_x, m_x, a_y, m_y = (rows[i : i + 1] for i in range(5))
        for r in range(OWN_T // FRAME_W):
            coord_y = row_coord(tgt * ROWS + qry * (OWN_T // FRAME_W) + r)
            shift = a_y * (coord_y - m_y)
            for k in range(0, FRAME_W, SUB):
                here = r * FRAME_W + k
                factor = jnp.exp2(top_ref[(d * OWN_T + here) // SUB] - top)
                slope, offset = (factor * a_x)[None], (factor * shift)[None]
                expo = e_ref[d * OWN_T + here : d * OWN_T + here + SUB, :].reshape(TILES, 8, NQ)
                away = (twice(cx_ref[k : k + SUB, :]) - m_x).reshape(TILES, 8, NQ)
                dscore = (expo * (away * slope + offset)).reshape(SUB, NQ).astype(BF16)
                add = jnp.dot(dscore, block, preferred_element_type=F32)
                out = pl.ds(here, SUB)
                if d == NG - 1:
                    gt_ref[out, :] = (gt_acc[out, :] + add).astype(BF16)
                else:
                    gt_acc[out, :] = add if d == 0 else gt_acc[out, :] + add

    for copy in v_copies:
        copy.wait_recv()
    piece = jnp.zeros((PIECE, NQ), F32)
    for i in range(NZ):
        s = slots[i]
        shift = grad_x * (s[5:6] - mean_x) + grad_y * (s[6:7] - mean_y)
        got = v_recv[i].astype(F32)
        piece = piece + jnp.exp2(s[4:5] - peak) * (got[:, :NQ] + shift * got[:, NQ:])
    part_y[NY] = piece * weight
    part_y[y] = part_y[NY]
    p_copies = [
        remote(part_y.at[NY], part_y.at[y], p_send.at[d], p_recv.at[d], at_y(d)) for d in Y_ORDER
    ]

    st_loc[2] = coef[qry]
    c_copies = [
        remote(st_loc.at[2], coef.at[qry], c_send.at[d], c_recv.at[d], at_g(d)) for d in G_ORDER
    ]

    more_expo(EARLY, NG - 1)
    target_block(0, qry, queries)

    for copy in p_copies:
        copy.wait_recv()
    whole = part_y[0]
    for i in range(1, NY):
        whole = whole + part_y[i]
    piece_z[NZ] = whole.astype(BF16)
    piece_z[z] = piece_z[NZ]
    f_copies = [
        remote(piece_z.at[NZ], piece_z.at[z], f_send.at[d], f_recv.at[d], at_z(d)) for d in Z_ORDER
    ]

    for i in range(NG - 1):
        c_copies[i].wait_recv()
        p = g_peer(NG - G_ORDER[i])
        target_block(i + 1, p, q_all[p])
    for copy in f_copies:
        copy.wait_recv()
    full = piece_z[0:NZ].reshape(CHANNELS, NQ).astype(F32)
    gq_ref[...] = full.T.astype(BF16)

    for copy in q_copies + y_copies + z_copies + v_copies + c_copies + p_copies + f_copies:
        copy.wait_send()


def copy_kernel(gq_in, gt_in, gq_out, gt_out, sem):
    copies = [
        pltpu.make_async_copy(gt_in, gt_out, sem.at[0]),
        pltpu.make_async_copy(gq_in, gq_out, sem.at[1]),
    ]
    for copy in copies:
        copy.start()
    for copy in copies:
        copy.wait()


def hand_over(grad_query, grad_target):
    vmem, anywhere = pl.BlockSpec(memory_space=pltpu.VMEM), pl.BlockSpec(memory_space=pl.ANY)
    return pl.pallas_call(
        copy_kernel,
        name="hand_over",
        out_shape=tuple(jax.ShapeDtypeStruct(a.shape, a.dtype) for a in (grad_query, grad_target)),
        in_specs=[vmem, vmem],
        out_specs=(anywhere, anywhere),
        scratch_shapes=[pltpu.SemaphoreType.DMA((2,))],
    )(grad_query, grad_target)


def body(query_feat, target_feat, flow_grad):
    vmem = pl.BlockSpec(memory_space=pltpu.VMEM)
    sems = pltpu.SemaphoreType.DMA
    grad_query, grad_target = pl.pallas_call(
        kernel,
        name="matching_backward",
        out_shape=(
            pltpu.VMEM((NQ, CHANNELS), BF16),
            pltpu.VMEM((OWN_T, CHANNELS), BF16),
        ),
        in_specs=[vmem, pl.BlockSpec(memory_space=pl.ANY), vmem],
        out_specs=(vmem, vmem),
        scratch_shapes=[
            pltpu.VMEM((NT, CHANNELS), BF16),
            pltpu.VMEM((NT, NQ), F32),
            pltpu.VMEM((FRAME_W, 128), F32),
            pltpu.VMEM((FRAME_W, NQ), F32),
            pltpu.VMEM((NT // SUB, 8, NQ), F32),
            pltpu.VMEM((NG * OWN_T // SUB, 8, NQ), F32),
            pltpu.VMEM((NG, NQ, CHANNELS), BF16),
            pltpu.VMEM((3, 8, NQ), F32),
            pltpu.VMEM((NY, 8, NQ), F32),
            pltpu.VMEM((NZ, 8, NQ), F32),
            pltpu.VMEM((NG, 8, NQ), F32),
            pltpu.VMEM((CHANNELS, 2 * NQ), BF16),
            pltpu.VMEM((NZ, PIECE, 2 * NQ), BF16),
            pltpu.VMEM((NY + 1, PIECE, NQ), F32),
            pltpu.VMEM((NZ + 1, PIECE, NQ), BF16),
            pltpu.VMEM((OWN_T, CHANNELS), F32),
            sems((GROUPS,)),
            sems((NG,)), sems((NG,)),
            sems((NY,)), sems((NY,)),
            sems((NZ,)), sems((NZ,)),
            sems((NG,)), sems((NG,)),
            sems((NZ,)), sems((NZ,)),
            sems((NY,)), sems((NY,)),
            sems((NZ,)), sems((NZ,)),
        ],
        compiler_params=pltpu.CompilerParams(
            collective_id=0, has_side_effects=True, vmem_limit_bytes=56 * 2**20
        ),
    )(query_feat, target_feat, flow_grad.T)
    return hand_over(grad_query, grad_target)


def solution(mesh):
    placed = (P("qry", None), P("tgt", None), P("qry", None))
    return jax.shard_map(
        body,
        mesh=mesh,
        in_specs=placed,
        out_specs=(P("qry", None), P(("tgt", "qry"), None)),
        check_vma=False,
    )
```

```python
import math

import jax
import jax.numpy as jnp
from jax import lax
from jax.experimental import pallas as pl
from jax.experimental.pallas import tpu as pltpu
from jax.sharding import PartitionSpec as P

MESH = pl.DeviceIdType.MESH
F32, BF16 = jnp.float32, jnp.bfloat16

CHANNELS = 128
FRAME_W = 1024
NQ = 256
NT = 16384
ROWS = NT // FRAME_W
OWN_T = 2048
NZ, NY, NG = 8, 4, 8
PIECE = CHANNELS // NZ
SUB = 256
TILES = SUB // 8
Z_ORDER = (4, 3, 5, 2, 6, 1, 7)
Y_ORDER = (2, 1, 3)
G_ORDER = (4, 3, 5, 2, 6, 1, 7)
EARLY = 3
GRAD_ROWS = 8
GROUPS = 4
SCALE = 1.0 / math.sqrt(CHANNELS)
LOG2 = SCALE * math.log2(math.e)


def twice(column):
    return jnp.concatenate([column, column], axis=1)


def scores_of(targets, queries):
    return lax.dot_general(targets, queries, (((1,), (1,)), ((), ())), preferred_element_type=F32)


def packed(rows):
    return jnp.concatenate([r[:, :128] for r in rows] + [r[:, 128:] for r in rows], axis=0)


def unpacked(tile):
    return jnp.concatenate([tile[0:4], tile[4:8]], axis=1)


def row_coord(row):
    return (2.0 * row.astype(F32) + 1.0) / FRAME_W - 1.0


def rows_at(start, count):
    return pl.ds(pl.multiple_of(start, count), count)


def kernel(
    q_ref, t_hbm, g_ref, gq_ref, gt_ref,
    t_ref, e_ref, cx_ref, xt_ref, peak_ref, top_ref, q_all, st_loc, st_y, st_z, st_l, c_own, coef, v_send, v_recv,
    part_y, piece_z, gt_acc,
    t_sem, q_send, q_recv, y_send, y_recv, z_send, z_recv, l_send, l_recv, c_send, c_recv,
    v_ssem, v_rsem, p_send, p_recv, f_send, f_recv,
):
    tgt, qry = lax.axis_index("tgt"), lax.axis_index("qry")
    z, y = tgt // NY, lax.rem(tgt, NY)

    def z_peer(d):
        return lax.rem(z + d, NZ)

    def y_peer(d):
        return lax.rem(y + d, NY)

    def g_peer(d):
        return lax.rem(qry + d, NG)

    def at_z(d):
        return (z_peer(d) * NY + y, qry)

    def at_y(d):
        return (z * NY + y_peer(d), qry)

    def at_g(d):
        return (tgt, g_peer(d))

    barrier = pltpu.get_barrier_semaphore()
    for d in range(1, NY):
        pl.semaphore_signal(barrier, inc=1, device_id=at_y(d), device_id_type=MESH)
    for d in range(1, NG):
        pl.semaphore_signal(barrier, inc=1, device_id=at_g(d), device_id_type=MESH)
    for d in range(1, NZ):
        pl.semaphore_signal(barrier, inc=1, device_id=at_z(d), device_id_type=MESH)

    def load(i):
        part = rows_at(i * (NT // GROUPS), NT // GROUPS)
        return pltpu.make_async_copy(t_hbm.at[part], t_ref.at[part], t_sem.at[i])

    for i in range(GROUPS):
        load(i).start()

    def remote(src, dst, ssem, rsem, where):
        copy = pltpu.make_async_remote_copy(
            src_ref=src, dst_ref=dst, send_sem=ssem, recv_sem=rsem, device_id=where, device_id_type=MESH
        )
        copy.start()
        return copy

    column = lax.broadcasted_iota(jnp.int32, (FRAME_W, 128), 0)
    cx_ref[...] = row_coord(column)
    queries = q_ref[...]
    grads = g_ref[...].astype(F32)
    grad_x, grad_y = grads[0:1], grads[1:2]

    def stats_row(b, carry):
        peak, total, sum_x, sum_y = carry
        coord_y = row_coord(tgt * ROWS + b)
        for k in range(0, FRAME_W, SUB):
            part = rows_at(b * FRAME_W + k, SUB)
            scores = scores_of(t_ref[part, :], queries).reshape(TILES, 8, NQ)
            top = jnp.maximum(peak, jnp.max(scores, axis=0) * LOG2)
            factor = jnp.exp2(peak - top)
            expo = jnp.exp2(scores * LOG2 - top[None])
            tot = expo[0]
            ahead = tot
            for i in range(1, TILES):
                tot = tot + expo[i]
                ahead = ahead + tot
            x_part = twice(cx_ref[k : k + 8, :]) * tot + (TILES * tot - ahead) * (16.0 / FRAME_W)
            total = total * factor + tot
            sum_x = sum_x * factor + x_part
            sum_y = sum_y * factor + coord_y * tot
            peak = top
            e_ref[part, :] = expo.reshape(SUB, NQ)
            peak_ref[b * (FRAME_W // SUB) + k // SUB] = top
        return peak, total, sum_x, sum_y

    def stats_group(i, carry):
        load(i).wait()
        for r in range(ROWS // GROUPS):
            carry = stats_row(i * (ROWS // GROUPS) + r, carry)
        return carry

    zeros = jnp.zeros((8, NQ), F32)
    carry = (jnp.full((8, NQ), -1e30, F32), zeros, zeros, zeros)
    carry = lax.fori_loop(0, 1, stats_group, carry)
    pl.semaphore_wait(barrier, NY - 1 + NG - 1 + NZ - 1)
    q_copies = [
        remote(q_ref, q_all.at[qry], q_send.at[d], q_recv.at[d], at_g(d)) for d in G_ORDER
    ]
    carry = lax.fori_loop(1, GROUPS, stats_group, carry)
    peak8, total8, x8, y8 = carry
    peak_l = jnp.max(peak8, axis=0, keepdims=True)
    factor8 = jnp.exp2(peak8 - peak_l)
    total_l = jnp.sum(total8 * factor8, axis=0, keepdims=True)
    sum_xl = jnp.sum(x8 * factor8, axis=0, keepdims=True)
    sum_yl = jnp.sum(y8 * factor8, axis=0, keepdims=True)
    mean_xl, mean_yl = sum_xl / total_l, sum_yl / total_l

    st_loc[0] = packed([peak_l, total_l, sum_xl, sum_yl])
    st_y[y] = st_loc[0]
    y_copies = [
        remote(st_loc.at[0], st_y.at[y], y_send.at[d], y_recv.at[d], at_y(d)) for d in Y_ORDER
    ]

    xt_ref[...] = (twice(cx_ref[...]) - mean_xl) * grad_x

    def grad_row(b, acc):
        coord_y = row_coord(tgt * ROWS + b)
        offset = grad_y * (coord_y - mean_yl)
        parts = []
        for k in range(0, FRAME_W, SUB):
            part = rows_at(b * FRAME_W + k, SUB)
            factor = jnp.exp2(peak_ref[b * (FRAME_W // SUB) + k // SUB] - peak_l)
            expo = (e_ref[part, :].reshape(TILES, 8, NQ) * factor[None]).reshape(SUB, NQ)
            inner = xt_ref[k : k + SUB, :] + offset
            parts.append(jnp.concatenate([(expo * inner).astype(BF16), expo.astype(BF16)], axis=1))
        block = t_ref[rows_at(b * FRAME_W, FRAME_W), :]
        return acc + lax.dot_general(
            block, jnp.concatenate(parts, axis=0), (((0,), (0,)), ((), ())), preferred_element_type=F32
        )

    def grad_group(i, acc):
        for r in range(GRAD_ROWS):
            acc = grad_row(i * GRAD_ROWS + r, acc)
        return acc

    v = lax.fori_loop(0, ROWS // GRAD_ROWS, grad_group, jnp.zeros((CHANNELS, 2 * NQ), F32))

    def merge(slots):
        slots = [unpacked(s) for s in slots]
        peak = slots[0][0:1]
        for s in slots[1:]:
            peak = jnp.maximum(peak, s[0:1])
        total = sum_x = sum_y = jnp.zeros((1, NQ), F32)
        for s in slots:
            factor = jnp.exp2(s[0:1] - peak)
            total = total + s[1:2] * factor
            sum_x = sum_x + s[2:3] * factor
            sum_y = sum_y + s[3:4] * factor
        return peak, total, sum_x, sum_y

    for copy in y_copies:
        copy.wait_recv()
    merged = merge([st_y[i] for i in range(NY)])
    st_loc[1] = packed(merged)
    st_z[z] = st_loc[1]
    z_copies = [
        remote(st_loc.at[1], st_z.at[z], z_send.at[d], z_recv.at[d], at_z(d)) for d in Z_ORDER
    ]
    st_loc[2] = packed([peak_l, mean_xl, mean_yl, mean_yl])
    st_l[z] = st_loc[2]
    l_copies = [
        remote(st_loc.at[2], st_l.at[z], l_send.at[d], l_recv.at[d], at_z(d)) for d in Z_ORDER
    ]
    v_send[...] = v.astype(BF16)
    v_recv[z] = v_send[rows_at(z * PIECE, PIECE), :]
    v_copies = [
        remote(
            v_send.at[rows_at(z_peer(d) * PIECE, PIECE)], v_recv.at[z], v_ssem.at[d], v_rsem.at[d], at_z(d)
        )
        for d in Z_ORDER
    ]

    def target_expo(d, block):
        for k in range(0, OWN_T, SUB):
            scores = scores_of(t_ref[rows_at(qry * OWN_T + k, SUB), :], block).reshape(TILES, 8, NQ)
            top = jnp.max(scores, axis=0) * LOG2
            expo = jnp.exp2(scores * LOG2 - top[None])
            e_ref[d * OWN_T + k : d * OWN_T + k + SUB, :] = expo.reshape(SUB, NQ)
            top_ref[(d * OWN_T + k) // SUB] = top

    def more_expo(first, last):
        for i in range(first, last):
            q_copies[i].wait_recv()
            target_expo(i + 1, q_all[g_peer(NG - G_ORDER[i])])

    target_expo(0, queries)
    more_expo(0, EARLY)

    for copy in z_copies:
        copy.wait_recv()
    peak, total, sum_x, sum_y = merge([st_z[i] for i in range(NZ)])
    mean_x, mean_y = sum_x / total, sum_y / total
    weight = SCALE / total
    coef[qry] = jnp.concatenate(
        [peak, grad_x * weight, mean_x, grad_y * weight, mean_y, zeros[0:3]], axis=0
    )

    def target_block(d, p, block):
        rows = coef[p]
        top, a_x, m_x, a_y, m_y = (rows[i : i + 1] for i in range(5))
        for r in range(OWN_T // FRAME_W):
            coord_y = row_coord(tgt * ROWS + qry * (OWN_T // FRAME_W) + r)
            shift = a_y * (coord_y - m_y)
            for k in range(0, FRAME_W, SUB):
                here = r * FRAME_W + k
                factor = jnp.exp2(top_ref[(d * OWN_T + here) // SUB] - top)
                slope, offset = (factor * a_x)[None], (factor * shift)[None]
                expo = e_ref[d * OWN_T + here : d * OWN_T + here + SUB, :].reshape(TILES, 8, NQ)
                away = (twice(cx_ref[k : k + SUB, :]) - m_x).reshape(TILES, 8, NQ)
                dscore = (expo * (away * slope + offset)).reshape(SUB, NQ).astype(BF16)
                add = jnp.dot(dscore, block, preferred_element_type=F32)
                out = pl.ds(here, SUB)
                if d == NG - 1:
                    gt_ref[out, :] = (gt_acc[out, :] + add).astype(BF16)
                else:
                    gt_acc[out, :] = add if d == 0 else gt_acc[out, :] + add

    for copy in l_copies + v_copies:
        copy.wait_recv()
    piece = jnp.zeros((PIECE, NQ), F32)
    for i in range(NZ):
        s = unpacked(st_l[i])
        shift = grad_x * (s[1:2] - mean_x) + grad_y * (s[2:3] - mean_y)
        got = v_recv[i].astype(F32)
        piece = piece + jnp.exp2(s[0:1] - peak) * (got[:, :NQ] + shift * got[:, NQ:])
    part_y[NY] = piece * weight
    part_y[y] = part_y[NY]
    p_copies = [
        remote(part_y.at[NY], part_y.at[y], p_send.at[d], p_recv.at[d], at_y(d)) for d in Y_ORDER
    ]

    c_own[...] = coef[qry]
    c_copies = [
        remote(c_own, coef.at[qry], c_send.at[d], c_recv.at[d], at_g(d)) for d in G_ORDER
    ]

    more_expo(EARLY, NG - 1)
    target_block(0, qry, queries)

    for copy in p_copies:
        copy.wait_recv()
    whole = part_y[0]
    for i in range(1, NY):
        whole = whole + part_y[i]
    piece_z[NZ] = whole.astype(BF16)
    piece_z[z] = piece_z[NZ]
    f_copies = [
        remote(piece_z.at[NZ], piece_z.at[z], f_send.at[d], f_recv.at[d], at_z(d)) for d in Z_ORDER
    ]

    for i in range(NG - 1):
        c_copies[i].wait_recv()
        p = g_peer(NG - G_ORDER[i])
        target_block(i + 1, p, q_all[p])
    for copy in f_copies:
        copy.wait_recv()
    full = piece_z[0:NZ].reshape(CHANNELS, NQ).astype(F32)
    gq_ref[...] = full.T.astype(BF16)

    for copy in q_copies + y_copies + z_copies + l_copies + v_copies + c_copies + p_copies + f_copies:
        copy.wait_send()


def copy_kernel(gq_in, gt_in, gq_out, gt_out, sem):
    copies = [
        pltpu.make_async_copy(gt_in, gt_out, sem.at[0]),
        pltpu.make_async_copy(gq_in, gq_out, sem.at[1]),
    ]
    for copy in copies:
        copy.start()
    for copy in copies:
        copy.wait()


def hand_over(grad_query, grad_target):
    vmem, anywhere = pl.BlockSpec(memory_space=pltpu.VMEM), pl.BlockSpec(memory_space=pl.ANY)
    return pl.pallas_call(
        copy_kernel,
        name="hand_over",
        out_shape=tuple(jax.ShapeDtypeStruct(a.shape, a.dtype) for a in (grad_query, grad_target)),
        in_specs=[vmem, vmem],
        out_specs=(anywhere, anywhere),
        scratch_shapes=[pltpu.SemaphoreType.DMA((2,))],
        compiler_params=pltpu.CompilerParams(vmem_limit_bytes=2**20),
    )(grad_query, grad_target)


def body(query_feat, target_feat, flow_grad):
    vmem = pl.BlockSpec(memory_space=pltpu.VMEM)
    sems = pltpu.SemaphoreType.DMA
    grad_query, grad_target = pl.pallas_call(
        kernel,
        name="matching_backward",
        out_shape=(
            pltpu.VMEM((NQ, CHANNELS), BF16),
            pltpu.VMEM((OWN_T, CHANNELS), BF16),
        ),
        in_specs=[vmem, pl.BlockSpec(memory_space=pl.ANY), vmem],
        out_specs=(vmem, vmem),
        scratch_shapes=[
            pltpu.VMEM((NT, CHANNELS), BF16),
            pltpu.VMEM((NT, NQ), F32),
            pltpu.VMEM((FRAME_W, 128), F32),
            pltpu.VMEM((FRAME_W, NQ), F32),
            pltpu.VMEM((NT // SUB, 8, NQ), F32),
            pltpu.VMEM((NG * OWN_T // SUB, 8, NQ), F32),
            pltpu.VMEM((NG, NQ, CHANNELS), BF16),
            pltpu.VMEM((3, 8, 128), F32),
            pltpu.VMEM((NY, 8, 128), F32),
            pltpu.VMEM((NZ, 8, 128), F32),
            pltpu.VMEM((NZ, 8, 128), F32),
            pltpu.VMEM((8, NQ), F32),
            pltpu.VMEM((NG, 8, NQ), F32),
            pltpu.VMEM((CHANNELS, 2 * NQ), BF16),
            pltpu.VMEM((NZ, PIECE, 2 * NQ), BF16),
            pltpu.VMEM((NY + 1, PIECE, NQ), F32),
            pltpu.VMEM((NZ + 1, PIECE, NQ), BF16),
            pltpu.VMEM((OWN_T, CHANNELS), F32),
            sems((GROUPS,)),
            sems((NG,)), sems((NG,)),
            sems((NY,)), sems((NY,)),
            sems((NZ,)), sems((NZ,)),
            sems((NZ,)), sems((NZ,)),
            sems((NG,)), sems((NG,)),
            sems((NZ,)), sems((NZ,)),
            sems((NY,)), sems((NY,)),
            sems((NZ,)), sems((NZ,)),
        ],
        compiler_params=pltpu.CompilerParams(
            collective_id=0, has_side_effects=True, vmem_limit_bytes=56 * 2**20
        ),
    )(query_feat, target_feat, flow_grad.T)
    return hand_over(grad_query, grad_target)


def solution(mesh):
    placed = (P("qry", None), P("tgt", None), P("qry", None))
    return jax.shard_map(
        body,
        mesh=mesh,
        in_specs=placed,
        out_specs=(P("qry", None), P(("tgt", "qry"), None)),
        check_vma=False,
    )
```

```python
import math

import jax
import jax.numpy as jnp
from jax import lax
from jax.experimental import pallas as pl
from jax.experimental.pallas import tpu as pltpu
from jax.sharding import PartitionSpec as P

MESH = pl.DeviceIdType.MESH
F32, BF16 = jnp.float32, jnp.bfloat16

CHANNELS = 128
FRAME_W = 1024
NQ = 256
NT = 16384
ROWS = NT // FRAME_W
OWN_T = 2048
NZ, NY, NG = 8, 4, 8
PIECE = CHANNELS // NZ
SUB = 256
TILES = SUB // 8
Z_ORDER = (4, 3, 5, 2, 6, 1, 7)
Y_ORDER = (2, 1, 3)
G_ORDER = (4, 3, 5, 2, 6, 1, 7)
EARLY = 3
GRAD_ROWS = 8
GROUPS = 4
SCALE = 1.0 / math.sqrt(CHANNELS)
LOG2 = SCALE * math.log2(math.e)


def twice(column):
    return jnp.concatenate([column, column], axis=1)


def scores_of(targets, queries):
    return lax.dot_general(targets, queries, (((1,), (1,)), ((), ())), preferred_element_type=F32)


def packed(rows):
    return jnp.concatenate([r[:, :128] for r in rows] + [r[:, 128:] for r in rows], axis=0)


def unpacked(tile):
    return jnp.concatenate([tile[0:4], tile[4:8]], axis=1)


def row_coord(row):
    return (2.0 * row.astype(F32) + 1.0) / FRAME_W - 1.0


def rows_at(start, count):
    return pl.ds(pl.multiple_of(start, count), count)


def kernel(
    q_hbm, t_hbm, g_hbm, gq_ref, gt_ref,
    q_ref, g_ref, t_ref, e_ref, cx_ref, xt_ref, peak_ref, top_ref, q_all, st_loc, st_y, st_z, st_l, c_own, coef, v_send, v_recv,
    part_y, piece_z, gt_acc,
    a_sem, t_sem, q_send, q_recv, y_send, y_recv, z_send, z_recv, l_send, l_recv, c_send, c_recv,
    v_ssem, v_rsem, p_send, p_recv, f_send, f_recv,
):
    tgt, qry = lax.axis_index("tgt"), lax.axis_index("qry")
    z, y = tgt // NY, lax.rem(tgt, NY)

    def z_peer(d):
        return lax.rem(z + d, NZ)

    def y_peer(d):
        return lax.rem(y + d, NY)

    def g_peer(d):
        return lax.rem(qry + d, NG)

    def at_z(d):
        return (z_peer(d) * NY + y, qry)

    def at_y(d):
        return (z * NY + y_peer(d), qry)

    def at_g(d):
        return (tgt, g_peer(d))

    q_load = pltpu.make_async_copy(q_hbm, q_ref, a_sem.at[0])
    g_load = pltpu.make_async_copy(g_hbm, g_ref, a_sem.at[1])
    q_load.start()

    def load(i):
        part = rows_at(i * (NT // GROUPS), NT // GROUPS)
        return pltpu.make_async_copy(t_hbm.at[part], t_ref.at[part], t_sem.at[i])

    load(0).start()
    g_load.start()
    for i in range(1, GROUPS):
        load(i).start()

    barrier = pltpu.get_barrier_semaphore()
    for d in range(1, NY):
        pl.semaphore_signal(barrier, inc=1, device_id=at_y(d), device_id_type=MESH)
    for d in range(1, NG):
        pl.semaphore_signal(barrier, inc=1, device_id=at_g(d), device_id_type=MESH)
    for d in range(1, NZ):
        pl.semaphore_signal(barrier, inc=1, device_id=at_z(d), device_id_type=MESH)

    def remote(src, dst, ssem, rsem, where):
        copy = pltpu.make_async_remote_copy(
            src_ref=src, dst_ref=dst, send_sem=ssem, recv_sem=rsem, device_id=where, device_id_type=MESH
        )
        copy.start()
        return copy

    column = lax.broadcasted_iota(jnp.int32, (FRAME_W, 128), 0)
    cx_ref[...] = row_coord(column)
    q_load.wait()
    queries = q_ref[...]

    def stats_row(b, carry):
        peak, total, sum_x, sum_y = carry
        coord_y = row_coord(tgt * ROWS + b)
        for k in range(0, FRAME_W, SUB):
            part = rows_at(b * FRAME_W + k, SUB)
            scores = scores_of(t_ref[part, :], queries).reshape(TILES, 8, NQ)
            top = jnp.maximum(peak, jnp.max(scores, axis=0) * LOG2)
            factor = jnp.exp2(peak - top)
            expo = jnp.exp2(scores * LOG2 - top[None])
            tot = expo[0]
            ahead = tot
            for i in range(1, TILES):
                tot = tot + expo[i]
                ahead = ahead + tot
            x_part = twice(cx_ref[k : k + 8, :]) * tot + (TILES * tot - ahead) * (16.0 / FRAME_W)
            total = total * factor + tot
            sum_x = sum_x * factor + x_part
            sum_y = sum_y * factor + coord_y * tot
            peak = top
            e_ref[part, :] = expo.reshape(SUB, NQ)
            peak_ref[b * (FRAME_W // SUB) + k // SUB] = top
        return peak, total, sum_x, sum_y

    def stats_group(i, carry):
        load(i).wait()
        for r in range(ROWS // GROUPS):
            carry = stats_row(i * (ROWS // GROUPS) + r, carry)
        return carry

    zeros = jnp.zeros((8, NQ), F32)
    carry = (jnp.full((8, NQ), -1e30, F32), zeros, zeros, zeros)
    carry = lax.fori_loop(0, 1, stats_group, carry)
    pl.semaphore_wait(barrier, NY - 1 + NG - 1 + NZ - 1)
    q_copies = [
        remote(q_ref, q_all.at[qry], q_send.at[d], q_recv.at[d], at_g(d)) for d in G_ORDER
    ]
    carry = lax.fori_loop(1, GROUPS, stats_group, carry)
    peak8, total8, x8, y8 = carry
    peak_l = jnp.max(peak8, axis=0, keepdims=True)
    factor8 = jnp.exp2(peak8 - peak_l)
    total_l = jnp.sum(total8 * factor8, axis=0, keepdims=True)
    sum_xl = jnp.sum(x8 * factor8, axis=0, keepdims=True)
    sum_yl = jnp.sum(y8 * factor8, axis=0, keepdims=True)
    mean_xl, mean_yl = sum_xl / total_l, sum_yl / total_l

    st_loc[0] = packed([peak_l, total_l, sum_xl, sum_yl])
    st_y[y] = st_loc[0]
    y_copies = [
        remote(st_loc.at[0], st_y.at[y], y_send.at[d], y_recv.at[d], at_y(d)) for d in Y_ORDER
    ]

    g_load.wait()
    grads = g_ref[...].astype(F32)
    grad_x, grad_y = grads[0:1], grads[1:2]

    xt_ref[...] = (twice(cx_ref[...]) - mean_xl) * grad_x

    def grad_row(b, acc):
        coord_y = row_coord(tgt * ROWS + b)
        offset = grad_y * (coord_y - mean_yl)
        parts = []
        for k in range(0, FRAME_W, SUB):
            part = rows_at(b * FRAME_W + k, SUB)
            factor = jnp.exp2(peak_ref[b * (FRAME_W // SUB) + k // SUB] - peak_l)
            expo = (e_ref[part, :].reshape(TILES, 8, NQ) * factor[None]).reshape(SUB, NQ)
            inner = xt_ref[k : k + SUB, :] + offset
            parts.append(jnp.concatenate([(expo * inner).astype(BF16), expo.astype(BF16)], axis=1))
        block = t_ref[rows_at(b * FRAME_W, FRAME_W), :]
        return acc + lax.dot_general(
            block, jnp.concatenate(parts, axis=0), (((0,), (0,)), ((), ())), preferred_element_type=F32
        )

    def grad_group(i, acc):
        for r in range(GRAD_ROWS):
            acc = grad_row(i * GRAD_ROWS + r, acc)
        return acc

    v = lax.fori_loop(0, ROWS // GRAD_ROWS, grad_group, jnp.zeros((CHANNELS, 2 * NQ), F32))

    def merge(slots):
        slots = [unpacked(s) for s in slots]
        peak = slots[0][0:1]
        for s in slots[1:]:
            peak = jnp.maximum(peak, s[0:1])
        total = sum_x = sum_y = jnp.zeros((1, NQ), F32)
        for s in slots:
            factor = jnp.exp2(s[0:1] - peak)
            total = total + s[1:2] * factor
            sum_x = sum_x + s[2:3] * factor
            sum_y = sum_y + s[3:4] * factor
        return peak, total, sum_x, sum_y

    for copy in y_copies:
        copy.wait_recv()
    merged = merge([st_y[i] for i in range(NY)])
    st_loc[1] = packed(merged)
    st_z[z] = st_loc[1]
    z_copies = [
        remote(st_loc.at[1], st_z.at[z], z_send.at[d], z_recv.at[d], at_z(d)) for d in Z_ORDER
    ]
    st_loc[2] = packed([peak_l, mean_xl, mean_yl, mean_yl])
    st_l[z] = st_loc[2]
    l_copies = [
        remote(st_loc.at[2], st_l.at[z], l_send.at[d], l_recv.at[d], at_z(d)) for d in Z_ORDER
    ]
    v_send[...] = v.astype(BF16)
    v_recv[z] = v_send[rows_at(z * PIECE, PIECE), :]
    v_copies = [
        remote(
            v_send.at[rows_at(z_peer(d) * PIECE, PIECE)], v_recv.at[z], v_ssem.at[d], v_rsem.at[d], at_z(d)
        )
        for d in Z_ORDER
    ]

    def target_expo(d, block):
        for k in range(0, OWN_T, SUB):
            scores = scores_of(t_ref[rows_at(qry * OWN_T + k, SUB), :], block).reshape(TILES, 8, NQ)
            top = jnp.max(scores, axis=0) * LOG2
            expo = jnp.exp2(scores * LOG2 - top[None])
            e_ref[d * OWN_T + k : d * OWN_T + k + SUB, :] = expo.reshape(SUB, NQ)
            top_ref[(d * OWN_T + k) // SUB] = top

    def more_expo(first, last):
        for i in range(first, last):
            q_copies[i].wait_recv()
            target_expo(i + 1, q_all[g_peer(NG - G_ORDER[i])])

    target_expo(0, queries)
    more_expo(0, EARLY)

    for copy in z_copies:
        copy.wait_recv()
    peak, total, sum_x, sum_y = merge([st_z[i] for i in range(NZ)])
    mean_x, mean_y = sum_x / total, sum_y / total
    weight = SCALE / total
    coef[qry] = jnp.concatenate(
        [peak, grad_x * weight, mean_x, grad_y * weight, mean_y, zeros[0:3]], axis=0
    )

    def target_block(d, p, block):
        rows = coef[p]
        top, a_x, m_x, a_y, m_y = (rows[i : i + 1] for i in range(5))
        for r in range(OWN_T // FRAME_W):
            coord_y = row_coord(tgt * ROWS + qry * (OWN_T // FRAME_W) + r)
            shift = a_y * (coord_y - m_y)
            for k in range(0, FRAME_W, SUB):
                here = r * FRAME_W + k
                factor = jnp.exp2(top_ref[(d * OWN_T + here) // SUB] - top)
                slope, offset = (factor * a_x)[None], (factor * shift)[None]
                expo = e_ref[d * OWN_T + here : d * OWN_T + here + SUB, :].reshape(TILES, 8, NQ)
                away = (twice(cx_ref[k : k + SUB, :]) - m_x).reshape(TILES, 8, NQ)
                dscore = (expo * (away * slope + offset)).reshape(SUB, NQ).astype(BF16)
                add = jnp.dot(dscore, block, preferred_element_type=F32)
                out = pl.ds(here, SUB)
                if d == NG - 1:
                    gt_ref[out, :] = (gt_acc[out, :] + add).astype(BF16)
                else:
                    gt_acc[out, :] = add if d == 0 else gt_acc[out, :] + add

    for copy in l_copies + v_copies:
        copy.wait_recv()
    piece = jnp.zeros((PIECE, NQ), F32)
    for i in range(NZ):
        s = unpacked(st_l[i])
        shift = grad_x * (s[1:2] - mean_x) + grad_y * (s[2:3] - mean_y)
        got = v_recv[i].astype(F32)
        piece = piece + jnp.exp2(s[0:1] - peak) * (got[:, :NQ] + shift * got[:, NQ:])
    part_y[NY] = piece * weight
    part_y[y] = part_y[NY]
    p_copies = [
        remote(part_y.at[NY], part_y.at[y], p_send.at[d], p_recv.at[d], at_y(d)) for d in Y_ORDER
    ]

    c_own[...] = coef[qry]
    c_copies = [
        remote(c_own, coef.at[qry], c_send.at[d], c_recv.at[d], at_g(d)) for d in G_ORDER
    ]

    more_expo(EARLY, NG - 1)
    target_block(0, qry, queries)

    for copy in p_copies:
        copy.wait_recv()
    whole = part_y[0]
    for i in range(1, NY):
        whole = whole + part_y[i]
    piece_z[NZ] = whole.astype(BF16)
    piece_z[z] = piece_z[NZ]
    f_copies = [
        remote(piece_z.at[NZ], piece_z.at[z], f_send.at[d], f_recv.at[d], at_z(d)) for d in Z_ORDER
    ]

    for i in range(NG - 1):
        c_copies[i].wait_recv()
        p = g_peer(NG - G_ORDER[i])
        target_block(i + 1, p, q_all[p])
    for copy in f_copies:
        copy.wait_recv()
    full = piece_z[0:NZ].reshape(CHANNELS, NQ).astype(F32)
    gq_ref[...] = full.T.astype(BF16)

    for copy in q_copies + y_copies + z_copies + l_copies + v_copies + c_copies + p_copies + f_copies:
        copy.wait_send()


def copy_kernel(gq_in, gt_in, gq_out, gt_out, sem):
    copies = [
        pltpu.make_async_copy(gt_in, gt_out, sem.at[0]),
        pltpu.make_async_copy(gq_in, gq_out, sem.at[1]),
    ]
    for copy in copies:
        copy.start()
    for copy in copies:
        copy.wait()


def hand_over(grad_query, grad_target):
    vmem, anywhere = pl.BlockSpec(memory_space=pltpu.VMEM), pl.BlockSpec(memory_space=pl.ANY)
    return pl.pallas_call(
        copy_kernel,
        name="hand_over",
        out_shape=tuple(jax.ShapeDtypeStruct(a.shape, a.dtype) for a in (grad_query, grad_target)),
        in_specs=[vmem, vmem],
        out_specs=(anywhere, anywhere),
        scratch_shapes=[pltpu.SemaphoreType.DMA((2,))],
        compiler_params=pltpu.CompilerParams(vmem_limit_bytes=2**20),
    )(grad_query, grad_target)


def body(query_feat, target_feat, flow_grad):
    vmem = pl.BlockSpec(memory_space=pltpu.VMEM)
    sems = pltpu.SemaphoreType.DMA
    grad_query, grad_target = pl.pallas_call(
        kernel,
        name="matching_backward",
        out_shape=(
            pltpu.VMEM((NQ, CHANNELS), BF16),
            pltpu.VMEM((OWN_T, CHANNELS), BF16),
        ),
        in_specs=[pl.BlockSpec(memory_space=pl.ANY)] * 3,
        out_specs=(vmem, vmem),
        scratch_shapes=[
            pltpu.VMEM((NQ, CHANNELS), BF16),
            pltpu.VMEM((2, NQ), BF16),
            pltpu.VMEM((NT, CHANNELS), BF16),
            pltpu.VMEM((NT, NQ), F32),
            pltpu.VMEM((FRAME_W, 128), F32),
            pltpu.VMEM((FRAME_W, NQ), F32),
            pltpu.VMEM((NT // SUB, 8, NQ), F32),
            pltpu.VMEM((NG * OWN_T // SUB, 8, NQ), F32),
            pltpu.VMEM((NG, NQ, CHANNELS), BF16),
            pltpu.VMEM((3, 8, 128), F32),
            pltpu.VMEM((NY, 8, 128), F32),
            pltpu.VMEM((NZ, 8, 128), F32),
            pltpu.VMEM((NZ, 8, 128), F32),
            pltpu.VMEM((8, NQ), F32),
            pltpu.VMEM((NG, 8, NQ), F32),
            pltpu.VMEM((CHANNELS, 2 * NQ), BF16),
            pltpu.VMEM((NZ, PIECE, 2 * NQ), BF16),
            pltpu.VMEM((NY + 1, PIECE, NQ), F32),
            pltpu.VMEM((NZ + 1, PIECE, NQ), BF16),
            pltpu.VMEM((OWN_T, CHANNELS), F32),
            sems((2,)),
            sems((GROUPS,)),
            sems((NG,)), sems((NG,)),
            sems((NY,)), sems((NY,)),
            sems((NZ,)), sems((NZ,)),
            sems((NZ,)), sems((NZ,)),
            sems((NG,)), sems((NG,)),
            sems((NZ,)), sems((NZ,)),
            sems((NY,)), sems((NY,)),
            sems((NZ,)), sems((NZ,)),
        ],
        compiler_params=pltpu.CompilerParams(
            collective_id=0, has_side_effects=True, vmem_limit_bytes=56 * 2**20
        ),
    )(query_feat, target_feat, flow_grad.T)
    return hand_over(grad_query, grad_target)


def solution(mesh):
    placed = (P("qry", None), P("tgt", None), P("qry", None))
    return jax.shard_map(
        body,
        mesh=mesh,
        in_specs=placed,
        out_specs=(P("qry", None), P(("tgt", "qry"), None)),
        check_vma=False,
    )
```

```python
import math

import jax
import jax.numpy as jnp
from jax import lax
from jax.experimental import pallas as pl
from jax.experimental.pallas import tpu as pltpu
from jax.sharding import PartitionSpec as P

MESH = pl.DeviceIdType.MESH
F32, BF16 = jnp.float32, jnp.bfloat16

CHANNELS = 128
FRAME_W = 1024
NQ = 256
NT = 16384
ROWS = NT // FRAME_W
OWN_T = 2048
NZ, NY, NG = 8, 4, 8
PIECE = CHANNELS // NZ
SUB = 256
TILES = SUB // 8
Z_ORDER = (4, 3, 5, 2, 6, 1, 7)
Y_ORDER = (2, 1, 3)
G_ORDER = (4, 3, 5, 2, 6, 1, 7)
EARLY = 3
GRAD_ROWS = 8
GROUPS = 4
SCALE = 1.0 / math.sqrt(CHANNELS)
LOG2 = SCALE * math.log2(math.e)


def twice(column):
    return jnp.concatenate([column, column], axis=1)


def scores_of(targets, queries):
    return lax.dot_general(targets, queries, (((1,), (1,)), ((), ())), preferred_element_type=F32)


def packed(rows):
    return jnp.concatenate([r[:, :128] for r in rows] + [r[:, 128:] for r in rows], axis=0)


def unpacked(tile):
    return jnp.concatenate([tile[0:4], tile[4:8]], axis=1)


def row_coord(row):
    return (2.0 * row.astype(F32) + 1.0) / FRAME_W - 1.0


def rows_at(start, count):
    return pl.ds(pl.multiple_of(start, count), count)


def kernel(
    q_hbm, t_hbm, g_hbm, gq_ref, gt_ref,
    q_ref, g_ref, t_ref, e_ref, cx_ref, xt_ref, peak_ref, top_ref, q_all, st_loc, st_y, st_z, c_own, coef, v_send, v_recv,
    part_y, piece_z, gt_acc,
    a_sem, t_sem, q_send, q_recv, y_send, y_recv, z_send, z_recv, c_send, c_recv,
    v_ssem, v_rsem, p_send, p_recv, f_send, f_recv,
):
    tgt, qry = lax.axis_index("tgt"), lax.axis_index("qry")
    z, y = tgt // NY, lax.rem(tgt, NY)

    def z_peer(d):
        return lax.rem(z + d, NZ)

    def y_peer(d):
        return lax.rem(y + d, NY)

    def g_peer(d):
        return lax.rem(qry + d, NG)

    def at_z(d):
        return (z_peer(d) * NY + y, qry)

    def at_y(d):
        return (z * NY + y_peer(d), qry)

    def at_g(d):
        return (tgt, g_peer(d))

    q_load = pltpu.make_async_copy(q_hbm, q_ref, a_sem.at[0])
    g_load = pltpu.make_async_copy(g_hbm, g_ref, a_sem.at[1])
    q_load.start()

    def load(i):
        part = rows_at(i * (NT // GROUPS), NT // GROUPS)
        return pltpu.make_async_copy(t_hbm.at[part], t_ref.at[part], t_sem.at[i])

    load(0).start()
    g_load.start()
    for i in range(1, GROUPS):
        load(i).start()

    barrier = pltpu.get_barrier_semaphore()
    for d in range(1, NY):
        pl.semaphore_signal(barrier, inc=1, device_id=at_y(d), device_id_type=MESH)
    for d in range(1, NG):
        pl.semaphore_signal(barrier, inc=1, device_id=at_g(d), device_id_type=MESH)
    for d in range(1, NZ):
        pl.semaphore_signal(barrier, inc=1, device_id=at_z(d), device_id_type=MESH)

    def remote(src, dst, ssem, rsem, where):
        copy = pltpu.make_async_remote_copy(
            src_ref=src, dst_ref=dst, send_sem=ssem, recv_sem=rsem, device_id=where, device_id_type=MESH
        )
        copy.start()
        return copy

    column = lax.broadcasted_iota(jnp.int32, (FRAME_W, 128), 0)
    cx_ref[...] = row_coord(column)
    q_load.wait()
    queries = q_ref[...]

    def stats_row(b, carry):
        peak, total, sum_x, sum_y = carry
        coord_y = row_coord(tgt * ROWS + b)
        for k in range(0, FRAME_W, SUB):
            part = rows_at(b * FRAME_W + k, SUB)
            scores = scores_of(t_ref[part, :], queries).reshape(TILES, 8, NQ)
            top = jnp.maximum(peak, jnp.max(scores, axis=0) * LOG2)
            factor = jnp.exp2(peak - top)
            expo = jnp.exp2(scores * LOG2 - top[None])
            tot = expo[0]
            ahead = tot
            for i in range(1, TILES):
                tot = tot + expo[i]
                ahead = ahead + tot
            x_part = twice(cx_ref[k : k + 8, :]) * tot + (TILES * tot - ahead) * (16.0 / FRAME_W)
            total = total * factor + tot
            sum_x = sum_x * factor + x_part
            sum_y = sum_y * factor + coord_y * tot
            peak = top
            e_ref[part, :] = expo.reshape(SUB, NQ)
            peak_ref[b * (FRAME_W // SUB) + k // SUB] = top
        return peak, total, sum_x, sum_y

    def stats_group(i, carry):
        load(i).wait()
        for r in range(ROWS // GROUPS):
            carry = stats_row(i * (ROWS // GROUPS) + r, carry)
        return carry

    zeros = jnp.zeros((8, NQ), F32)
    carry = (jnp.full((8, NQ), -1e30, F32), zeros, zeros, zeros)
    carry = lax.fori_loop(0, 1, stats_group, carry)
    pl.semaphore_wait(barrier, NY - 1 + NG - 1 + NZ - 1)
    q_copies = [
        remote(q_ref, q_all.at[qry], q_send.at[d], q_recv.at[d], at_g(d)) for d in G_ORDER
    ]
    carry = lax.fori_loop(1, GROUPS, stats_group, carry)
    peak8, total8, x8, y8 = carry
    peak_l = jnp.max(peak8, axis=0, keepdims=True)
    factor8 = jnp.exp2(peak8 - peak_l)
    total_l = jnp.sum(total8 * factor8, axis=0, keepdims=True)
    sum_xl = jnp.sum(x8 * factor8, axis=0, keepdims=True)
    sum_yl = jnp.sum(y8 * factor8, axis=0, keepdims=True)
    mean_xl, mean_yl = sum_xl / total_l, sum_yl / total_l

    def merge(slots):
        slots = [unpacked(s) for s in slots]
        peak = slots[0][0:1]
        for s in slots[1:]:
            peak = jnp.maximum(peak, s[0:1])
        total = sum_x = sum_y = jnp.zeros((1, NQ), F32)
        for s in slots:
            factor = jnp.exp2(s[0:1] - peak)
            total = total + s[1:2] * factor
            sum_x = sum_x + s[2:3] * factor
            sum_y = sum_y + s[3:4] * factor
        return peak, total, sum_x, sum_y

    st_loc[0] = packed([peak_l, total_l, sum_xl, sum_yl])
    st_z[z] = st_loc[0]
    z_copies = [
        remote(st_loc.at[0], st_z.at[z], z_send.at[d], z_recv.at[d], at_z(d)) for d in Z_ORDER
    ]

    g_load.wait()
    grads = g_ref[...].astype(F32)
    grad_x, grad_y = grads[0:1], grads[1:2]

    xt_ref[...] = (twice(cx_ref[...]) - mean_xl) * grad_x

    def grad_row(b, acc):
        coord_y = row_coord(tgt * ROWS + b)
        offset = grad_y * (coord_y - mean_yl)
        parts = []
        for k in range(0, FRAME_W, SUB):
            part = rows_at(b * FRAME_W + k, SUB)
            factor = jnp.exp2(peak_ref[b * (FRAME_W // SUB) + k // SUB] - peak_l)
            expo = (e_ref[part, :].reshape(TILES, 8, NQ) * factor[None]).reshape(SUB, NQ)
            inner = xt_ref[k : k + SUB, :] + offset
            parts.append(jnp.concatenate([(expo * inner).astype(BF16), expo.astype(BF16)], axis=1))
        block = t_ref[rows_at(b * FRAME_W, FRAME_W), :]
        return acc + lax.dot_general(
            block, jnp.concatenate(parts, axis=0), (((0,), (0,)), ((), ())), preferred_element_type=F32
        )

    def grad_group(i, acc):
        for r in range(GRAD_ROWS):
            acc = grad_row(i * GRAD_ROWS + r, acc)
        return acc

    v = lax.fori_loop(0, ROWS // GRAD_ROWS, grad_group, jnp.zeros((CHANNELS, 2 * NQ), F32))


    v_send[...] = v.astype(BF16)
    v_recv[z] = v_send[rows_at(z * PIECE, PIECE), :]
    v_copies = [
        remote(
            v_send.at[rows_at(z_peer(d) * PIECE, PIECE)], v_recv.at[z], v_ssem.at[d], v_rsem.at[d], at_z(d)
        )
        for d in Z_ORDER
    ]

    def target_expo(d, block):
        for k in range(0, OWN_T, SUB):
            scores = scores_of(t_ref[rows_at(qry * OWN_T + k, SUB), :], block).reshape(TILES, 8, NQ)
            top = jnp.max(scores, axis=0) * LOG2
            expo = jnp.exp2(scores * LOG2 - top[None])
            e_ref[d * OWN_T + k : d * OWN_T + k + SUB, :] = expo.reshape(SUB, NQ)
            top_ref[(d * OWN_T + k) // SUB] = top

    def more_expo(first, last):
        for i in range(first, last):
            q_copies[i].wait_recv()
            target_expo(i + 1, q_all[g_peer(NG - G_ORDER[i])])

    target_expo(0, queries)

    for copy in z_copies:
        copy.wait_recv()
    st_loc[1] = packed(merge([st_z[i] for i in range(NZ)]))
    st_y[y] = st_loc[1]
    y_copies = [
        remote(st_loc.at[1], st_y.at[y], y_send.at[d], y_recv.at[d], at_y(d)) for d in Y_ORDER
    ]
    more_expo(0, EARLY)

    for copy in y_copies:
        copy.wait_recv()
    peak, total, sum_x, sum_y = merge([st_y[i] for i in range(NY)])
    mean_x, mean_y = sum_x / total, sum_y / total
    weight = SCALE / total
    coef[qry] = jnp.concatenate(
        [peak, grad_x * weight, mean_x, grad_y * weight, mean_y, zeros[0:3]], axis=0
    )

    def target_block(d, p, block):
        rows = coef[p]
        top, a_x, m_x, a_y, m_y = (rows[i : i + 1] for i in range(5))
        for r in range(OWN_T // FRAME_W):
            coord_y = row_coord(tgt * ROWS + qry * (OWN_T // FRAME_W) + r)
            shift = a_y * (coord_y - m_y)
            for k in range(0, FRAME_W, SUB):
                here = r * FRAME_W + k
                factor = jnp.exp2(top_ref[(d * OWN_T + here) // SUB] - top)
                slope, offset = (factor * a_x)[None], (factor * shift)[None]
                expo = e_ref[d * OWN_T + here : d * OWN_T + here + SUB, :].reshape(TILES, 8, NQ)
                away = (twice(cx_ref[k : k + SUB, :]) - m_x).reshape(TILES, 8, NQ)
                dscore = (expo * (away * slope + offset)).reshape(SUB, NQ).astype(BF16)
                add = jnp.dot(dscore, block, preferred_element_type=F32)
                out = pl.ds(here, SUB)
                if d == NG - 1:
                    gt_ref[out, :] = (gt_acc[out, :] + add).astype(BF16)
                else:
                    gt_acc[out, :] = add if d == 0 else gt_acc[out, :] + add

    for copy in v_copies:
        copy.wait_recv()
    piece = jnp.zeros((PIECE, NQ), F32)
    for i in range(NZ):
        s = unpacked(st_z[i])
        shift = grad_x * (s[2:3] / s[1:2] - mean_x) + grad_y * (s[3:4] / s[1:2] - mean_y)
        got = v_recv[i].astype(F32)
        piece = piece + jnp.exp2(s[0:1] - peak) * (got[:, :NQ] + shift * got[:, NQ:])
    part_y[NY] = piece * weight
    part_y[y] = part_y[NY]
    p_copies = [
        remote(part_y.at[NY], part_y.at[y], p_send.at[d], p_recv.at[d], at_y(d)) for d in Y_ORDER
    ]

    c_own[...] = coef[qry]
    c_copies = [
        remote(c_own, coef.at[qry], c_send.at[d], c_recv.at[d], at_g(d)) for d in G_ORDER
    ]

    more_expo(EARLY, NG - 1)
    target_block(0, qry, queries)

    for copy in p_copies:
        copy.wait_recv()
    whole = part_y[0]
    for i in range(1, NY):
        whole = whole + part_y[i]
    piece_z[NZ] = whole.astype(BF16)
    piece_z[z] = piece_z[NZ]
    f_copies = [
        remote(piece_z.at[NZ], piece_z.at[z], f_send.at[d], f_recv.at[d], at_z(d)) for d in Z_ORDER
    ]

    for i in range(NG - 1):
        c_copies[i].wait_recv()
        p = g_peer(NG - G_ORDER[i])
        target_block(i + 1, p, q_all[p])
    for copy in f_copies:
        copy.wait_recv()
    full = piece_z[0:NZ].reshape(CHANNELS, NQ).astype(F32)
    gq_ref[...] = full.T.astype(BF16)

    for copy in q_copies + y_copies + z_copies + v_copies + c_copies + p_copies + f_copies:
        copy.wait_send()


def copy_kernel(gq_in, gt_in, gq_out, gt_out, sem):
    copies = [
        pltpu.make_async_copy(gt_in, gt_out, sem.at[0]),
        pltpu.make_async_copy(gq_in, gq_out, sem.at[1]),
    ]
    for copy in copies:
        copy.start()
    for copy in copies:
        copy.wait()


def hand_over(grad_query, grad_target):
    vmem, anywhere = pl.BlockSpec(memory_space=pltpu.VMEM), pl.BlockSpec(memory_space=pl.ANY)
    return pl.pallas_call(
        copy_kernel,
        name="hand_over",
        out_shape=tuple(jax.ShapeDtypeStruct(a.shape, a.dtype) for a in (grad_query, grad_target)),
        in_specs=[vmem, vmem],
        out_specs=(anywhere, anywhere),
        scratch_shapes=[pltpu.SemaphoreType.DMA((2,))],
        compiler_params=pltpu.CompilerParams(vmem_limit_bytes=2**20),
    )(grad_query, grad_target)


def body(query_feat, target_feat, flow_grad):
    vmem = pl.BlockSpec(memory_space=pltpu.VMEM)
    sems = pltpu.SemaphoreType.DMA
    grad_query, grad_target = pl.pallas_call(
        kernel,
        name="matching_backward",
        out_shape=(
            pltpu.VMEM((NQ, CHANNELS), BF16),
            pltpu.VMEM((OWN_T, CHANNELS), BF16),
        ),
        in_specs=[pl.BlockSpec(memory_space=pl.ANY)] * 3,
        out_specs=(vmem, vmem),
        scratch_shapes=[
            pltpu.VMEM((NQ, CHANNELS), BF16),
            pltpu.VMEM((2, NQ), BF16),
            pltpu.VMEM((NT, CHANNELS), BF16),
            pltpu.VMEM((NT, NQ), F32),
            pltpu.VMEM((FRAME_W, 128), F32),
            pltpu.VMEM((FRAME_W, NQ), F32),
            pltpu.VMEM((NT // SUB, 8, NQ), F32),
            pltpu.VMEM((NG * OWN_T // SUB, 8, NQ), F32),
            pltpu.VMEM((NG, NQ, CHANNELS), BF16),
            pltpu.VMEM((2, 8, 128), F32),
            pltpu.VMEM((NY, 8, 128), F32),
            pltpu.VMEM((NZ, 8, 128), F32),
            pltpu.VMEM((8, NQ), F32),
            pltpu.VMEM((NG, 8, NQ), F32),
            pltpu.VMEM((CHANNELS, 2 * NQ), BF16),
            pltpu.VMEM((NZ, PIECE, 2 * NQ), BF16),
            pltpu.VMEM((NY + 1, PIECE, NQ), F32),
            pltpu.VMEM((NZ + 1, PIECE, NQ), BF16),
            pltpu.VMEM((OWN_T, CHANNELS), F32),
            sems((2,)),
            sems((GROUPS,)),
            sems((NG,)), sems((NG,)),
            sems((NY,)), sems((NY,)),
            sems((NZ,)), sems((NZ,)),
            sems((NG,)), sems((NG,)),
            sems((NZ,)), sems((NZ,)),
            sems((NY,)), sems((NY,)),
            sems((NZ,)), sems((NZ,)),
        ],
        compiler_params=pltpu.CompilerParams(
            collective_id=0, has_side_effects=True, vmem_limit_bytes=56 * 2**20
        ),
    )(query_feat, target_feat, flow_grad.T)
    return hand_over(grad_query, grad_target)


def solution(mesh):
    placed = (P("qry", None), P("tgt", None), P("qry", None))
    return jax.shard_map(
        body,
        mesh=mesh,
        in_specs=placed,
        out_specs=(P("qry", None), P(("tgt", "qry"), None)),
        check_vma=False,
    )
```

```python
import math

import jax
import jax.numpy as jnp
from jax import lax
from jax.experimental import pallas as pl
from jax.experimental.pallas import tpu as pltpu
from jax.sharding import PartitionSpec as P

MESH = pl.DeviceIdType.MESH
F32, BF16 = jnp.float32, jnp.bfloat16

CHANNELS = 128
FRAME_W = 1024
NQ = 256
NT = 16384
ROWS = NT // FRAME_W
OWN_T = 2048
NZ, NY, NG = 8, 4, 8
PIECE = CHANNELS // NZ
SUB = 256
TILES = SUB // 8
Z_ORDER = (4, 3, 5, 2, 6, 1, 7)
Y_ORDER = (2, 1, 3)
G_ORDER = (4, 3, 5, 2, 6, 1, 7)
EARLY = 3
GRAD_ROWS = 16
GROUPS = 4
SCALE = 1.0 / math.sqrt(CHANNELS)
LOG2 = SCALE * math.log2(math.e)


def twice(column):
    return jnp.concatenate([column, column], axis=1)


def scores_of(targets, queries):
    return lax.dot_general(targets, queries, (((1,), (1,)), ((), ())), preferred_element_type=F32)


def packed(rows):
    return jnp.concatenate([r[:, :128] for r in rows] + [r[:, 128:] for r in rows], axis=0)


def unpacked(tile):
    return jnp.concatenate([tile[0:4], tile[4:8]], axis=1)


def row_coord(row):
    return (2.0 * row.astype(F32) + 1.0) / FRAME_W - 1.0


def rows_at(start, count):
    return pl.ds(pl.multiple_of(start, count), count)


def kernel(
    q_hbm, t_hbm, g_hbm, gq_ref, gt_ref,
    q_ref, g_ref, t_ref, e_ref, cx_ref, xt_ref, peak_ref, top_ref, q_all, st_loc, st_y, st_z, c_own, coef, v_send, v_recv,
    part_y, piece_z, gt_acc,
    a_sem, t_sem, q_send, q_recv, y_send, y_recv, z_send, z_recv, c_send, c_recv,
    v_ssem, v_rsem, p_send, p_recv, f_send, f_recv,
):
    tgt, qry = lax.axis_index("tgt"), lax.axis_index("qry")
    z, y = tgt // NY, lax.rem(tgt, NY)

    def z_peer(d):
        return lax.rem(z + d, NZ)

    def y_peer(d):
        return lax.rem(y + d, NY)

    def g_peer(d):
        return lax.rem(qry + d, NG)

    def at_z(d):
        return (z_peer(d) * NY + y, qry)

    def at_y(d):
        return (z * NY + y_peer(d), qry)

    def at_g(d):
        return (tgt, g_peer(d))

    q_load = pltpu.make_async_copy(q_hbm, q_ref, a_sem.at[0])
    g_load = pltpu.make_async_copy(g_hbm, g_ref, a_sem.at[1])
    q_load.start()

    def load(i):
        part = rows_at(i * (NT // GROUPS), NT // GROUPS)
        return pltpu.make_async_copy(t_hbm.at[part], t_ref.at[part], t_sem.at[i])

    load(0).start()
    g_load.start()
    for i in range(1, GROUPS):
        load(i).start()

    barrier = pltpu.get_barrier_semaphore()
    for d in range(1, NY):
        pl.semaphore_signal(barrier, inc=1, device_id=at_y(d), device_id_type=MESH)
    for d in range(1, NG):
        pl.semaphore_signal(barrier, inc=1, device_id=at_g(d), device_id_type=MESH)
    for d in range(1, NZ):
        pl.semaphore_signal(barrier, inc=1, device_id=at_z(d), device_id_type=MESH)

    def remote(src, dst, ssem, rsem, where):
        copy = pltpu.make_async_remote_copy(
            src_ref=src, dst_ref=dst, send_sem=ssem, recv_sem=rsem, device_id=where, device_id_type=MESH
        )
        copy.start()
        return copy

    column = lax.broadcasted_iota(jnp.int32, (FRAME_W, 128), 0)
    cx_ref[...] = row_coord(column)
    q_load.wait()
    queries = q_ref[...]

    def stats_row(b, carry):
        peak, total, sum_x, sum_y = carry
        coord_y = row_coord(tgt * ROWS + b)
        for k in range(0, FRAME_W, SUB):
            part = rows_at(b * FRAME_W + k, SUB)
            scores = scores_of(t_ref[part, :], queries).reshape(TILES, 8, NQ)
            top = jnp.maximum(peak, jnp.max(scores, axis=0) * LOG2)
            factor = jnp.exp2(peak - top)
            expo = jnp.exp2(scores * LOG2 - top[None])
            tot = expo[0]
            ahead = tot
            for i in range(1, TILES):
                tot = tot + expo[i]
                ahead = ahead + tot
            x_part = twice(cx_ref[k : k + 8, :]) * tot + (TILES * tot - ahead) * (16.0 / FRAME_W)
            total = total * factor + tot
            sum_x = sum_x * factor + x_part
            sum_y = sum_y * factor + coord_y * tot
            peak = top
            e_ref[part, :] = expo.reshape(SUB, NQ)
            peak_ref[b * (FRAME_W // SUB) + k // SUB] = top
        return peak, total, sum_x, sum_y

    def stats_group(i, carry):
        load(i).wait()
        for r in range(ROWS // GROUPS):
            carry = stats_row(i * (ROWS // GROUPS) + r, carry)
        return carry

    zeros = jnp.zeros((8, NQ), F32)
    carry = (jnp.full((8, NQ), -1e30, F32), zeros, zeros, zeros)
    carry = lax.fori_loop(0, 1, stats_group, carry)
    pl.semaphore_wait(barrier, NY - 1 + NG - 1 + NZ - 1)
    q_copies = [
        remote(q_ref, q_all.at[qry], q_send.at[d], q_recv.at[d], at_g(d)) for d in G_ORDER
    ]
    carry = lax.fori_loop(1, GROUPS, stats_group, carry)
    peak8, total8, x8, y8 = carry
    peak_l = jnp.max(peak8, axis=0, keepdims=True)
    factor8 = jnp.exp2(peak8 - peak_l)
    total_l = jnp.sum(total8 * factor8, axis=0, keepdims=True)
    sum_xl = jnp.sum(x8 * factor8, axis=0, keepdims=True)
    sum_yl = jnp.sum(y8 * factor8, axis=0, keepdims=True)
    mean_xl, mean_yl = sum_xl / total_l, sum_yl / total_l

    def merge(slots):
        slots = [unpacked(s) for s in slots]
        peak = slots[0][0:1]
        for s in slots[1:]:
            peak = jnp.maximum(peak, s[0:1])
        total = sum_x = sum_y = jnp.zeros((1, NQ), F32)
        for s in slots:
            factor = jnp.exp2(s[0:1] - peak)
            total = total + s[1:2] * factor
            sum_x = sum_x + s[2:3] * factor
            sum_y = sum_y + s[3:4] * factor
        return peak, total, sum_x, sum_y

    st_loc[0] = packed([peak_l, total_l, sum_xl, sum_yl])
    st_z[z] = st_loc[0]
    z_copies = [
        remote(st_loc.at[0], st_z.at[z], z_send.at[d], z_recv.at[d], at_z(d)) for d in Z_ORDER
    ]

    g_load.wait()
    grads = g_ref[...].astype(F32)
    grad_x, grad_y = grads[0:1], grads[1:2]

    xt_ref[...] = (twice(cx_ref[...]) - mean_xl) * grad_x

    def grad_row(b, acc):
        coord_y = row_coord(tgt * ROWS + b)
        offset = grad_y * (coord_y - mean_yl)
        parts = []
        for k in range(0, FRAME_W, SUB):
            part = rows_at(b * FRAME_W + k, SUB)
            factor = jnp.exp2(peak_ref[b * (FRAME_W // SUB) + k // SUB] - peak_l)
            expo = (e_ref[part, :].reshape(TILES, 8, NQ) * factor[None]).reshape(SUB, NQ)
            inner = xt_ref[k : k + SUB, :] + offset
            parts.append(jnp.concatenate([(expo * inner).astype(BF16), expo.astype(BF16)], axis=1))
        block = t_ref[rows_at(b * FRAME_W, FRAME_W), :]
        return acc + lax.dot_general(
            block, jnp.concatenate(parts, axis=0), (((0,), (0,)), ((), ())), preferred_element_type=F32
        )

    def grad_group(i, acc):
        for r in range(GRAD_ROWS):
            acc = grad_row(i * GRAD_ROWS + r, acc)
        return acc

    v = lax.fori_loop(0, ROWS // GRAD_ROWS, grad_group, jnp.zeros((CHANNELS, 2 * NQ), F32))


    v_send[...] = v.astype(BF16)
    v_copies = [
        remote(
            v_send.at[rows_at(z_peer(d) * PIECE, PIECE)], v_recv.at[z], v_ssem.at[d], v_rsem.at[d], at_z(d)
        )
        for d in Z_ORDER
    ]

    v_recv[z] = v_send[rows_at(z * PIECE, PIECE), :]

    def target_expo(d, block):
        for k in range(0, OWN_T, SUB):
            scores = scores_of(t_ref[rows_at(qry * OWN_T + k, SUB), :], block).reshape(TILES, 8, NQ)
            top = jnp.max(scores, axis=0) * LOG2
            expo = jnp.exp2(scores * LOG2 - top[None])
            e_ref[d * OWN_T + k : d * OWN_T + k + SUB, :] = expo.reshape(SUB, NQ)
            top_ref[(d * OWN_T + k) // SUB] = top

    def more_expo(first, last):
        for i in range(first, last):
            q_copies[i].wait_recv()
            target_expo(i + 1, q_all[g_peer(NG - G_ORDER[i])])

    target_expo(0, queries)

    for copy in z_copies:
        copy.wait_recv()
    st_loc[1] = packed(merge([st_z[i] for i in range(NZ)]))
    st_y[y] = st_loc[1]
    y_copies = [
        remote(st_loc.at[1], st_y.at[y], y_send.at[d], y_recv.at[d], at_y(d)) for d in Y_ORDER
    ]
    more_expo(0, EARLY)

    for copy in y_copies:
        copy.wait_recv()
    peak, total, sum_x, sum_y = merge([st_y[i] for i in range(NY)])
    mean_x, mean_y = sum_x / total, sum_y / total
    weight = SCALE / total
    coef[qry] = jnp.concatenate(
        [peak, grad_x * weight, mean_x, grad_y * weight, mean_y, zeros[0:3]], axis=0
    )

    def target_block(d, p, block):
        rows = coef[p]
        top, a_x, m_x, a_y, m_y = (rows[i : i + 1] for i in range(5))
        for r in range(OWN_T // FRAME_W):
            coord_y = row_coord(tgt * ROWS + qry * (OWN_T // FRAME_W) + r)
            shift = a_y * (coord_y - m_y)
            for k in range(0, FRAME_W, SUB):
                here = r * FRAME_W + k
                factor = jnp.exp2(top_ref[(d * OWN_T + here) // SUB] - top)
                slope, offset = (factor * a_x)[None], (factor * shift)[None]
                expo = e_ref[d * OWN_T + here : d * OWN_T + here + SUB, :].reshape(TILES, 8, NQ)
                away = (twice(cx_ref[k : k + SUB, :]) - m_x).reshape(TILES, 8, NQ)
                dscore = (expo * (away * slope + offset)).reshape(SUB, NQ).astype(BF16)
                add = jnp.dot(dscore, block, preferred_element_type=F32)
                out = pl.ds(here, SUB)
                if d == NG - 1:
                    gt_ref[out, :] = (gt_acc[out, :] + add).astype(BF16)
                else:
                    gt_acc[out, :] = add if d == 0 else gt_acc[out, :] + add

    for copy in v_copies:
        copy.wait_recv()
    piece = jnp.zeros((PIECE, NQ), F32)
    for i in range(NZ):
        s = unpacked(st_z[i])
        shift = grad_x * (s[2:3] / s[1:2] - mean_x) + grad_y * (s[3:4] / s[1:2] - mean_y)
        got = v_recv[i].astype(F32)
        piece = piece + jnp.exp2(s[0:1] - peak) * (got[:, :NQ] + shift * got[:, NQ:])
    part_y[NY] = piece * weight
    part_y[y] = part_y[NY]
    p_copies = [
        remote(part_y.at[NY], part_y.at[y], p_send.at[d], p_recv.at[d], at_y(d)) for d in Y_ORDER
    ]

    c_own[...] = coef[qry]
    c_copies = [
        remote(c_own, coef.at[qry], c_send.at[d], c_recv.at[d], at_g(d)) for d in G_ORDER
    ]

    more_expo(EARLY, NG - 1)
    target_block(0, qry, queries)

    for copy in p_copies:
        copy.wait_recv()
    whole = part_y[0]
    for i in range(1, NY):
        whole = whole + part_y[i]
    piece_z[NZ] = whole.astype(BF16)
    piece_z[z] = piece_z[NZ]
    f_copies = [
        remote(piece_z.at[NZ], piece_z.at[z], f_send.at[d], f_recv.at[d], at_z(d)) for d in Z_ORDER
    ]

    for i in range(NG - 1):
        c_copies[i].wait_recv()
        p = g_peer(NG - G_ORDER[i])
        target_block(i + 1, p, q_all[p])
    for copy in f_copies:
        copy.wait_recv()
    full = piece_z[0:NZ].reshape(CHANNELS, NQ).astype(F32)
    gq_ref[...] = full.T.astype(BF16)

    for copy in q_copies + y_copies + z_copies + v_copies + c_copies + p_copies + f_copies:
        copy.wait_send()


def copy_kernel(gq_in, gt_in, gq_out, gt_out, sem):
    copies = [
        pltpu.make_async_copy(gt_in, gt_out, sem.at[0]),
        pltpu.make_async_copy(gq_in, gq_out, sem.at[1]),
    ]
    for copy in copies:
        copy.start()
    for copy in copies:
        copy.wait()


def hand_over(grad_query, grad_target):
    vmem, anywhere = pl.BlockSpec(memory_space=pltpu.VMEM), pl.BlockSpec(memory_space=pl.ANY)
    return pl.pallas_call(
        copy_kernel,
        name="hand_over",
        out_shape=tuple(jax.ShapeDtypeStruct(a.shape, a.dtype) for a in (grad_query, grad_target)),
        in_specs=[vmem, vmem],
        out_specs=(anywhere, anywhere),
        scratch_shapes=[pltpu.SemaphoreType.DMA((2,))],
        compiler_params=pltpu.CompilerParams(vmem_limit_bytes=2**20),
    )(grad_query, grad_target)


def body(query_feat, target_feat, flow_grad):
    vmem = pl.BlockSpec(memory_space=pltpu.VMEM)
    sems = pltpu.SemaphoreType.DMA
    grad_query, grad_target = pl.pallas_call(
        kernel,
        name="matching_backward",
        out_shape=(
            pltpu.VMEM((NQ, CHANNELS), BF16),
            pltpu.VMEM((OWN_T, CHANNELS), BF16),
        ),
        in_specs=[pl.BlockSpec(memory_space=pl.ANY)] * 3,
        out_specs=(vmem, vmem),
        scratch_shapes=[
            pltpu.VMEM((NQ, CHANNELS), BF16),
            pltpu.VMEM((2, NQ), BF16),
            pltpu.VMEM((NT, CHANNELS), BF16),
            pltpu.VMEM((NT, NQ), F32),
            pltpu.VMEM((FRAME_W, 128), F32),
            pltpu.VMEM((FRAME_W, NQ), F32),
            pltpu.VMEM((NT // SUB, 8, NQ), F32),
            pltpu.VMEM((NG * OWN_T // SUB, 8, NQ), F32),
            pltpu.VMEM((NG, NQ, CHANNELS), BF16),
            pltpu.VMEM((2, 8, 128), F32),
            pltpu.VMEM((NY, 8, 128), F32),
            pltpu.VMEM((NZ, 8, 128), F32),
            pltpu.VMEM((8, NQ), F32),
            pltpu.VMEM((NG, 8, NQ), F32),
            pltpu.VMEM((CHANNELS, 2 * NQ), BF16),
            pltpu.VMEM((NZ, PIECE, 2 * NQ), BF16),
            pltpu.VMEM((NY + 1, PIECE, NQ), F32),
            pltpu.VMEM((NZ + 1, PIECE, NQ), BF16),
            pltpu.VMEM((OWN_T, CHANNELS), F32),
            sems((2,)),
            sems((GROUPS,)),
            sems((NG,)), sems((NG,)),
            sems((NY,)), sems((NY,)),
            sems((NZ,)), sems((NZ,)),
            sems((NG,)), sems((NG,)),
            sems((NZ,)), sems((NZ,)),
            sems((NY,)), sems((NY,)),
            sems((NZ,)), sems((NZ,)),
        ],
        compiler_params=pltpu.CompilerParams(
            collective_id=0, has_side_effects=True, vmem_limit_bytes=56 * 2**20
        ),
    )(query_feat, target_feat, flow_grad.T)
    return hand_over(grad_query, grad_target)


def solution(mesh):
    placed = (P("qry", None), P("tgt", None), P("qry", None))
    return jax.shard_map(
        body,
        mesh=mesh,
        in_specs=placed,
        out_specs=(P("qry", None), P(("tgt", "qry"), None)),
        check_vma=False,
    )
```
